32 devices in a mesh: img: 8 (over z, y), grp: 4 (over x, core).
Axes of the slice: x: 2, y: 2, z: 4, core: 2. Of those that a mesh axis runs over, the one named last changes fastest.
Arguments:
- image_in: bfloat16 [1024, 1792], P('img', 'grp'), may hold values from -6 to 6
- text_in: bfloat16 [1024, 1152], P('img', 'grp'), may hold values from -6 to 6
- image_gain: float32 [1792], replicated, may hold values from 0.25 to 1.75
- text_gain: float32 [1152], replicated, may hold values from 0.25 to 1.75
- image_up: bfloat16 [1792, 7680], P('img', 'grp'), may hold values from -0.125 to 0.125
- image_down: bfloat16 [7680, 1792], P('grp', 'img'), may hold values from -0.0625 to 0.0625
- text_up: bfloat16 [1152, 2560], P(None, 'grp'), may hold values from -0.1875 to 0.1875
- text_down: bfloat16 [2560, 1152], P('grp'), may hold values from -0.125 to 0.125
- image_head: bfloat16 [1792, 1152], P('grp'), may hold values from -0.041666667 to 2
- log_scale: float32 [1], replicated, may hold values from 2.4 to 2.9
- bias: float32 [1], replicated, may hold values from -9 to -6
Outputs:
- image_grad: bfloat16 [1024, 1792], P('img', 'grp')
- text_grad: bfloat16 [1024, 1152], P('img', 'grp')
The draws below stay inside these ranges and needn't reach their ends.
All inputs are finite; a program needn't handle non-finite values.
Results may differ from the reference program's by a relative error of at most 0.0082.
Values may be sent and summed in bfloat16 or wider, within the bound.
No kernel may reach another device: no remote copies, remote signals or barrier semaphores. Data moves between devices by JAX's collectives and lax.ppermute only.
A program may use at most 128 MiB of HBM per device.

```python
import jax
import jax.numpy as jnp
from jax import lax

DI = 1792
FI = 7680
DT = 1152
FT = 2560
ROWS = 128
BATCH = 1024
N_IMG = 8


def shared_rows(key):
    cluster_total = max(DT // 8, 2)
    centres = jax.random.normal(jax.random.fold_in(key, 21), (cluster_total, DI), jnp.float32)
    members = jax.random.randint(jax.random.fold_in(key, 22), (BATCH,), 0, cluster_total)
    strength = jax.random.uniform(jax.random.fold_in(key, 23), (BATCH, 1), jnp.float32, 0.7, 1.3)
    own_part = jax.random.normal(jax.random.fold_in(key, 24), (BATCH, DI), jnp.float32)
    return 0.7 * own_part + strength * centres[members]


def draw_image_in(key, part):
    common = shared_rows(key)
    key = jax.random.fold_in(key, 3)
    values = common + 0.4 * jax.random.normal(key, (BATCH, DI), jnp.float32)
    return jnp.clip(values, -6.0, 6.0).astype(jnp.bfloat16)


def draw_text_in(key, part):
    common = shared_rows(key)[:, :DT]
    key = jax.random.fold_in(key, 4)
    values = common + 0.4 * jax.random.normal(key, (BATCH, DT), jnp.float32)
    return jnp.clip(values, -6.0, 6.0).astype(jnp.bfloat16)


def draw_image_head(key, part):
    key = jax.random.fold_in(key, 5)
    noise_limit = 0.99 * 3.0 / (DI // 32 + 16)
    noise_part = jax.random.uniform(key, (DI, DT), jnp.float32, -noise_limit, noise_limit)
    diagonal = 1.0 + jax.random.uniform(jax.random.fold_in(key, 9), (DI, DT), jnp.float32)
    on_diagonal = jnp.arange(DI)[:, None] == jnp.arange(DT)[None, :]
    return jnp.where(on_diagonal, diagonal, noise_part).astype(jnp.bfloat16)


def block_scale(own_key, shape, pieces, low, top_value):
    level, own = 1.0, jax.random.fold_in(own_key, 6)
    for axis_at, parts in pieces:
        draws = jnp.exp(jax.random.uniform(jax.random.fold_in(own, axis_at), (parts,), jnp.float32, low / len(pieces), top_value / len(pieces)))
        level = level * jnp.repeat(draws, shape[axis_at] // parts).reshape([-1 if axis == axis_at else 1 for axis in range(len(shape))])
    return level


def centred(stream_key, extent, spread, reach, split=(), kind=jnp.bfloat16):
    result = jax.random.normal(stream_key, extent, jnp.float32) * spread
    if len(split) > 0:
        result = block_scale(stream_key, extent, split, -0.22, 0.18) * result
    return jnp.clip(result, min=-reach, max=reach).astype(kind)


def setup_inputs(seed: int = 0) -> dict:
    keys = jax.random.split(jax.random.key(seed), 12)
    image_in = draw_image_in(jax.random.fold_in(keys[11], 71), 0)
    text_in = draw_text_in(jax.random.fold_in(keys[11], 71), 0)
    image_gain = jnp.clip(1.0 + 0.15 * jax.random.normal(keys[2], (DI,), jnp.float32), 0.25, 1.75)
    text_gain = jnp.clip(1.0 + 0.15 * jax.random.normal(keys[3], (DT,), jnp.float32), 0.25, 1.75)
    image_up = centred(keys[4], (DI, FI), DI ** -0.5, 0.125, ((0, 8), (1, 4)))
    image_down = centred(keys[5], (FI, DI), FI ** -0.5, 0.0625, ((0, 4), (1, 8)))
    text_up = centred(keys[6], (DT, FT), DT ** -0.5, 0.1875, ((1, 4),))
    text_down = centred(keys[7], (FT, DT), FT ** -0.5, 0.125, ((0, 4),))
    image_head = draw_image_head(jax.random.fold_in(keys[11], 71), 0)
    log_scale = jnp.clip(jax.random.uniform(keys[9], (1,), jnp.float32, 2.4, 2.9), 2.4, 2.9)
    bias = jnp.clip(jax.random.uniform(keys[10], (1,), jnp.float32, -9.0, -6.0), -9.0, -6.0)
    return {"image_in": image_in, "text_in": text_in, "image_gain": image_gain, "text_gain": text_gain, "image_up": image_up, "image_down": image_down, "text_up": text_up, "text_down": text_down, "image_head": image_head, "log_scale": log_scale, "bias": bias}


EPS = 1e-06

def layer_norm(rows, gain):
    rows = rows.astype(jnp.float32)
    mean = lax.optimization_barrier(jnp.mean(rows, axis=1, keepdims=True))
    centered = rows - mean
    inverse = lax.rsqrt(lax.optimization_barrier(jnp.mean(centered * centered, axis=1, keepdims=True)) + EPS)
    normed = centered * inverse
    return (normed, inverse, (normed * gain).astype(jnp.bfloat16))

def tower(rows, gain, up_weight, down_weight):
    normed, inverse, scaled = layer_norm(rows, gain)
    before = jnp.dot(scaled, up_weight, preferred_element_type=jnp.float32)
    hidden = jax.nn.gelu(before, approximate=True).astype(jnp.bfloat16)
    branch = jnp.dot(hidden, down_weight, preferred_element_type=jnp.float32)
    return (normed, inverse, before, branch)

def tower_back(upstream, normed, inverse, before, gain, up_weight, down_weight):
    grad_hidden = jnp.dot(upstream, down_weight.T, preferred_element_type=jnp.float32)
    _, gelu_back = jax.vjp(lambda value: jax.nn.gelu(value, approximate=True), before)
    grad_before = gelu_back(grad_hidden)[0].astype(jnp.bfloat16)
    grad_scaled = jnp.dot(grad_before, up_weight.T, preferred_element_type=jnp.float32)
    scaled_grad = grad_scaled * gain
    first = lax.optimization_barrier(jnp.mean(scaled_grad, axis=1, keepdims=True))
    second = lax.optimization_barrier(jnp.mean(scaled_grad * normed, axis=1, keepdims=True))
    return inverse * (scaled_grad - first - normed * second)

def unit_rows(embed):
    inv = lax.rsqrt(lax.optimization_barrier(jnp.sum(embed * embed, axis=1, keepdims=True)) + EPS)
    return (inv, (embed * inv).astype(jnp.bfloat16))

def unit_back(embed, inv, grad):
    along = lax.optimization_barrier(jnp.sum(embed * grad, axis=1, keepdims=True))
    return inv * (grad - embed * (inv * inv) * along)

def reference(image_in, text_in, image_gain, text_gain, image_up, image_down, text_up, text_down, image_head, log_scale, bias):
    total = image_in.shape[0]
    img_normed, img_inverse, img_before, img_branch = tower(image_in, image_gain, image_up, image_down)
    image_mid16 = (image_in.astype(jnp.float32) + img_branch).astype(jnp.bfloat16)
    image_embed = jnp.dot(image_mid16, image_head, preferred_element_type=jnp.float32)
    img_inv, image_unit = unit_rows(image_embed)
    txt_normed, txt_inverse, txt_before, txt_branch = tower(text_in, text_gain, text_up, text_down)
    text_embed = text_in.astype(jnp.float32) + txt_branch
    txt_inv, text_unit = unit_rows(text_embed)
    scale = jnp.exp(log_scale[0])
    shift = bias[0]
    text_ids = jnp.arange(total, dtype=jnp.int32)

    def block_step(accum, index):
        start = (index * ROWS).astype(jnp.int32)
        units = lax.dynamic_slice_in_dim(image_unit, start, ROWS, 0)
        cosine = jnp.dot(units, text_unit.T, preferred_element_type=jnp.float32)
        logits = scale * cosine + shift
        image_ids = start + jnp.arange(ROWS, dtype=jnp.int32)
        same = (image_ids[:, None] == text_ids[None, :]).astype(jnp.float32)
        pull = (jax.nn.sigmoid(logits) - same).astype(jnp.bfloat16)
        grad_img = scale * jnp.dot(pull, text_unit, preferred_element_type=jnp.float32)
        accum = accum + scale * jnp.dot(pull.T, units, preferred_element_type=jnp.float32)
        return (accum, grad_img)
    grad_text_unit, blocks = lax.scan(block_step, jnp.zeros((total, DT), jnp.float32), jnp.arange(N_IMG, dtype=jnp.int32))
    grad_image_unit = blocks.reshape(total, DT)
    grad_img_embed16 = unit_back(image_embed, img_inv, grad_image_unit).astype(jnp.bfloat16)
    grad_mid = jnp.dot(grad_img_embed16, image_head.T, preferred_element_type=jnp.float32)
    grad_mid16 = grad_mid.astype(jnp.bfloat16)
    img_back = tower_back(grad_mid16, img_normed, img_inverse, img_before, image_gain, image_up, image_down)
    image_grad = (grad_mid + img_back).astype(jnp.bfloat16)
    grad_txt_embed16 = unit_back(text_embed, txt_inv, grad_text_unit).astype(jnp.bfloat16)
    txt_back = tower_back(grad_txt_embed16, txt_normed, txt_inverse, txt_before, text_gain, text_up, text_down)
    text_grad = (grad_txt_embed16.astype(jnp.float32) + txt_back).astype(jnp.bfloat16)
    return (image_grad, text_grad)
```

```python
import jax
import jax.numpy as jnp
from jax import lax
from jax.sharding import PartitionSpec as P

EPS = 1e-06
BF16 = jnp.bfloat16
F32 = jnp.float32


def swap(value, axis, flip):
    return lax.ppermute(value, axis, [(i, i ^ flip) for i in range(lax.axis_size(axis))])


def pick(index, options):
    chosen = options[0]
    for at, option in enumerate(options[1:], 1):
        chosen = jnp.where(index == at, option, chosen)
    return chosen


def place(parts, index, flips):
    whole = jnp.zeros((len(flips),) + parts[0].shape, parts[0].dtype)
    for part, flip in zip(parts, flips):
        whole = lax.dynamic_update_index_in_dim(whole, part, index ^ flip, 0)
    return whole


def dot(left, right, left_dim, right_dim):
    dims = (((left_dim,), (right_dim,)), ((), ()))
    return lax.dot_general(left, right, dims, preferred_element_type=F32)


def gather_hidden(shard, img):
    members = lax.axis_size("img")
    top = members // 2
    half = shard.shape[1] // 2
    low, high = shard[:, :half], shard[:, half:]
    upper = img >= top
    own = jnp.where(upper, high, low)
    other = swap(jnp.where(upper, low, high), "img", top)
    held, flips = jnp.stack([own, other]), [0, top]
    bit = top // 2
    while bit > 2:
        held = jnp.concatenate([held, swap(held, "img", bit)])
        flips = flips + [flip ^ bit for flip in flips]
        bit //= 2
    middle = len(flips) // 2
    by_one, by_two = swap(held, "img", 1), swap(held, "img", 2)
    both = [swap(by_one[:middle], "img", 2), swap(by_two[middle:], "img", 1)]
    blocks, places = [], []
    for array, extra in ((held, 0), (by_one, 1), (by_two, 2)):
        blocks += [array[at] for at in range(len(flips))]
        places += [flip ^ extra for flip in flips]
    blocks += [array[at] for array in both for at in range(middle)]
    places += [flip ^ 3 for flip in flips]
    return place(blocks, img, places).reshape(members * shard.shape[0], half)


def stats(rows):
    rows = rows.astype(F32)
    mean = jnp.mean(rows, axis=-1, keepdims=True)
    centered = rows - mean
    inverse = lax.rsqrt(jnp.mean(centered * centered, axis=-1, keepdims=True) + EPS)
    return mean, inverse


def scatter_rows(partial, grp):
    x, core = grp // 2, grp % 2
    lead = partial.shape[:-3]
    split = partial.reshape(lead + (2, 2) + partial.shape[-2:])
    axis = len(lead) + 1
    keep = lax.dynamic_index_in_dim(split, core, axis, False)
    send = lax.dynamic_index_in_dim(split, 1 - core, axis, False)
    total = keep + swap(send.astype(BF16), "grp", 1).astype(F32)
    keep = lax.dynamic_index_in_dim(total, x, axis - 1, False)
    send = lax.dynamic_index_in_dim(total, 1 - x, axis - 1, False)
    return keep + swap(send.astype(BF16), "grp", 2).astype(F32)


def packed(data, sums):
    high = lax.reduce_precision(sums, 8, 7)
    columns = [data.astype(BF16), high.astype(BF16), (sums - high).astype(BF16)]
    used = data.shape[-1] + 4
    columns.append(jnp.zeros(data.shape[:-1] + (-used % 128,), BF16))
    return jnp.concatenate(columns, axis=-1)


def unpacked(payload, cols):
    payload = payload.astype(F32)
    high, low = payload[..., cols : cols + 2], payload[..., cols + 2 : cols + 4]
    return payload[..., :cols], high + low


def scatter_cols(partial, gain, normed, grp, upper, top):
    x, core = grp // 2, grp % 2
    cols = partial.shape[-1] // 4
    scaled_grad = partial * gain
    sums = jnp.stack([jnp.sum(scaled_grad, -1), jnp.sum(scaled_grad * normed, -1)], -1)
    blocks = [partial[..., at * cols : (at + 1) * cols] for at in range(4)]
    keep = [jnp.where(core == 1, blocks[at + 1], blocks[at]) for at in (0, 2)]
    send = [jnp.where(core == 1, blocks[at], blocks[at + 1]) for at in (0, 2)]
    got = swap(jnp.stack([packed(part, sums) for part in send]), "grp", 1)
    pairs = [unpacked(got[at], cols) for at in (0, 1)]
    keep = [part + pair[0] for part, pair in zip(keep, pairs)]
    sums = sums + pairs[0][1]
    send = jnp.where(x == 1, keep[0], keep[1])
    keep = jnp.where(x == 1, keep[1], keep[0])
    data, more = unpacked(swap(packed(send, sums), "grp", 2), cols)
    keep, sums = keep + data, sums + more
    if top:
        rows = keep.shape[0] // 2
        keep, sums = keep.reshape(2, rows, cols), sums.reshape(2, rows, 2)
        send = jnp.where(upper, packed(keep[0], sums[0]), packed(keep[1], sums[1]))
        data, more = unpacked(swap(send, "img", top), cols)
        keep = jnp.where(upper, keep[1], keep[0]) + data
        sums = jnp.where(upper, sums[1], sums[0]) + more
    return keep, sums


def norm_back(grad, sums, rows, mean, inverse, gain, grp, features):
    cols = rows.shape[1]
    own_gain = lax.dynamic_slice_in_dim(gain, grp * cols, cols, 0)
    normed = (rows.astype(F32) - mean) * inverse
    first, second = sums[:, 0:1] / features, sums[:, 1:2] / features
    return inverse * (grad * own_gain - first - normed * second)


def unit_rows(embed):
    inv = lax.rsqrt(jnp.sum(embed * embed, axis=1, keepdims=True) + EPS)
    return inv, (embed * inv).astype(BF16)


def unit_back(embed, inv, grad):
    along = jnp.sum(embed * grad, axis=1, keepdims=True)
    return inv * (grad - embed * (inv * inv) * along)


def gelu16(before):
    return jax.nn.gelu(before, approximate=True).astype(BF16)


def gelu_back16(before, grad):
    _, back = jax.vjp(lambda value: jax.nn.gelu(value, approximate=True), before)
    return back(grad)[0].astype(BF16)


def shards(
    image_in,
    text_in,
    image_gain,
    text_gain,
    image_up,
    image_down,
    text_up,
    text_down,
    image_head,
    log_scale,
    bias,
):
    img, grp = lax.axis_index("img"), lax.axis_index("grp")
    members = lax.axis_size("img")
    top = members // 2
    upper = img >= top
    rows, image_cols = image_in.shape
    quarter = rows // 4
    text_cols = text_in.shape[1]
    image_features, text_features = image_cols * 4, text_cols * 4
    embed_width = image_head.shape[1]
    scale = jnp.exp(log_scale[0])
    shift = bias[0]

    with jax.named_scope("weights"):
        up = gather_hidden(image_up, img)
        down = gather_hidden(image_down.T, img)

    with jax.named_scope("image_rows"):
        far_in = swap(image_in, "img", top)
        near = lax.all_gather(image_in, "grp", axis=1, tiled=True)
        far = lax.all_gather(far_in, "grp", axis=1, tiled=True)
        whole = jnp.concatenate([jnp.where(upper, far, near), jnp.where(upper, near, far)])
        mean, inverse = stats(whole)
        normed = (whole.astype(F32) - mean) * inverse
        scaled = (normed * image_gain).astype(BF16)

    with jax.named_scope("text_forward"):
        text_whole = lax.all_gather(text_in, "grp", axis=1, tiled=True)
        text_mean, text_inverse = stats(text_whole)
        text_normed = (text_whole.astype(F32) - text_mean) * text_inverse
        text_before = dot((text_normed * text_gain).astype(BF16), text_up, 1, 0)
        text_branch = dot(gelu16(text_before), text_down, 1, 0)
        text_sum = scatter_rows(text_branch.reshape(4, quarter, text_features), grp)
        own_rows = lax.dynamic_slice_in_dim(text_whole, grp * quarter, quarter, 0)
        text_embed = own_rows.astype(F32) + text_sum
        text_inv, text_unit = unit_rows(text_embed)

    with jax.named_scope("text_units"):
        held, flips, bit = text_unit[None], [0], 1
        while bit < members:
            held = jnp.concatenate([held, swap(held, "img", bit)])
            flips = flips + [flip ^ bit for flip in flips]
            bit *= 2
        share = place([held[at] for at in range(members)], img, flips)
        share = share.reshape(members * quarter, embed_width)
        pair = jnp.stack([share, swap(share, "grp", 2)])
        every = jnp.concatenate([pair, swap(pair, "grp", 1)])
        every_flips = [0, 2, 1, 3]
        every_text = every.reshape(4 * members * quarter, embed_width)
        at = jnp.arange(members * quarter, dtype=jnp.int32)
        share_ids = at // quarter * rows + at % quarter
        text_ids = jnp.concatenate([share_ids + (grp ^ flip) * quarter for flip in every_flips])

    with jax.named_scope("head"):
        pair = jnp.stack([image_head, swap(image_head, "grp", 2)])
        pairs = [pair, swap(pair, "grp", 1)]
        blocks = [block[at] for block in pairs for at in (0, 1)]
        head = place(blocks, grp, every_flips).reshape(image_features, embed_width)

    with jax.named_scope("image_forward"):
        before = dot(scaled, up, 1, 0)
        branch = dot(gelu16(before), down, 1, 1)
        branch = scatter_rows(branch.reshape(2, 4, quarter, image_features), grp)
        send = jnp.where(upper, branch[0], branch[1]).astype(BF16)
        branch = jnp.where(upper, branch[1], branch[0]) + swap(send, "img", top).astype(F32)
        start = upper.astype(jnp.int32) * rows + grp * quarter
        image_mid = lax.dynamic_slice_in_dim(whole, start, quarter, 0).astype(F32) + branch
        image_embed = dot(image_mid.astype(BF16), head, 1, 0)
        image_inv, image_unit = unit_rows(image_embed)

    with jax.named_scope("image_loss"):
        image_ids = img * rows + grp * quarter + jnp.arange(quarter, dtype=jnp.int32)
        logits = scale * dot(image_unit, every_text, 1, 1) + shift
        same = (image_ids[:, None] == text_ids[None, :]).astype(F32)
        pull = (jax.nn.sigmoid(logits) - same).astype(BF16)
        grad_image_unit = scale * dot(pull, every_text, 1, 0)
        grad_embed16 = unit_back(image_embed, image_inv, grad_image_unit).astype(BF16)
        grad_mid16 = dot(grad_embed16, head, 1, 1).astype(BF16)

    with jax.named_scope("image_backward"):
        far_grad = swap(grad_mid16, "img", top)
        near = lax.all_gather(grad_mid16, "grp", axis=0, tiled=True)
        far = lax.all_gather(far_grad, "grp", axis=0, tiled=True)
        upstream = jnp.concatenate([jnp.where(upper, far, near), jnp.where(upper, near, far)])
        grad_before = gelu_back16(before, dot(upstream, down, 1, 0))
        partial = dot(grad_before, up, 1, 1)
        grad, sums = scatter_cols(partial, image_gain, normed, grp, upper, top)
        own_mean = jnp.where(upper, mean[rows:], mean[:rows])
        own_inverse = jnp.where(upper, inverse[rows:], inverse[:rows])
        back = norm_back(
            grad, sums, image_in, own_mean, own_inverse, image_gain, grp, image_features
        )
        own_grad = pick(grp, [near[:, at * image_cols : (at + 1) * image_cols] for at in range(4)])
        image_grad = (own_grad.astype(F32) + back).astype(BF16)

    with jax.named_scope("text_loss"):
        image_units = lax.all_gather(image_unit, "grp", axis=0, tiled=True)
        logits = scale * dot(image_units, share, 1, 1) + shift
        group_ids = img * rows + jnp.arange(rows, dtype=jnp.int32)
        same = (group_ids[:, None] == (share_ids + grp * quarter)[None, :]).astype(F32)
        pull = (jax.nn.sigmoid(logits) - same).astype(BF16)
        partial = (scale * dot(pull, image_units, 0, 0)).astype(BF16)
        partial = partial.reshape(members, quarter, embed_width)
        parts = lax.all_to_all(partial, "img", split_axis=0, concat_axis=0, tiled=True)
        grad_text_unit = jnp.sum(parts.astype(F32), axis=0)
        grad_text16 = unit_back(text_embed, text_inv, grad_text_unit).astype(BF16)

    with jax.named_scope("text_backward"):
        upstream = lax.all_gather(grad_text16, "grp", axis=0, tiled=True)
        grad_before = gelu_back16(text_before, dot(upstream, text_down, 1, 1))
        partial = dot(grad_before, text_up, 1, 1)
        grad, sums = scatter_cols(partial, text_gain, text_normed, grp, upper, 0)
        back = norm_back(
            grad, sums, text_in, text_mean, text_inverse, text_gain, grp, text_features
        )
        own_grad = pick(
            grp, [upstream[:, at * text_cols : (at + 1) * text_cols] for at in range(4)]
        )
        text_grad = (own_grad.astype(F32) + back).astype(BF16)
    return (image_grad, text_grad)


def solution(mesh):
    in_specs = (
        P("img", "grp"),
        P("img", "grp"),
        P(),
        P(),
        P("img", "grp"),
        P("grp", "img"),
        P(None, "grp"),
        P("grp", None),
        P("grp", None),
        P(),
        P(),
    )
    out_specs = (P("img", "grp"), P("img", "grp"))
    return jax.shard_map(shards, mesh=mesh, in_specs=in_specs, out_specs=out_specs, check_vma=False)
```

```python
import jax
import jax.numpy as jnp
from jax import lax
from jax.experimental import pallas as pl
from jax.experimental.pallas import tpu as pltpu
from jax.sharding import PartitionSpec as P

EPS = 1e-06
BF16 = jnp.bfloat16
F32 = jnp.float32
FLIPS = (0, 2, 1, 3)
GELU_C = 0.7978845608028654
GELU_A = 0.044715
VMEM = pl.BlockSpec(memory_space=pltpu.VMEM)
SMEM = pl.BlockSpec(memory_space=pltpu.SMEM)
PARAMS = pltpu.CompilerParams(vmem_limit_bytes=40 * 1024 * 1024)


def swap(value, axis, flip):
    return lax.ppermute(value, axis, [(i, i ^ flip) for i in range(lax.axis_size(axis))])


def place(parts, index, flips):
    whole = jnp.zeros((len(flips),) + parts[0].shape, parts[0].dtype)
    for part, flip in zip(parts, flips):
        whole = lax.dynamic_update_index_in_dim(whole, part, index ^ flip, 0)
    return whole


def dot(left, right, left_dim, right_dim):
    dims = (((left_dim,), (right_dim,)), ((), ()))
    return lax.dot_general(left, right, dims, preferred_element_type=F32)


def take(array, index, axis=0):
    return lax.dynamic_index_in_dim(array, index, axis, False)


def halves(shard, img):
    half = shard.shape[1] // 2
    low, high = shard[:, :half], shard[:, half:]
    upper = img >= lax.axis_size("img") // 2
    return jnp.where(upper, high, low), jnp.where(upper, low, high)


def widen(block, img):
    members = lax.axis_size("img")
    held, flips, bit = block[None], [0], 4
    while bit < members // 2:
        held = jnp.concatenate([held, swap(held, "img", bit)])
        flips = flips + [flip ^ (bit // 4) for flip in flips]
        bit *= 2
    if len(flips) > 1:
        middle = img // 4 % (members // 8)
        held = place([held[at] for at in range(len(flips))], middle, flips)
    return held.reshape(-1, block.shape[1])


def blocked(natural):
    members, rows, width = natural.shape
    if members == 8:
        return natural
    split = natural.reshape(2, members // 8, 4, rows, width)
    return split.transpose(0, 2, 3, 1, 4).reshape(8, rows, members // 8 * width)


def in_order(blocks, members):
    if members == 8:
        return blocks
    rows, width = blocks.shape[1], blocks.shape[2] * 8 // members
    split = blocks.reshape(2, 4, rows, members // 8, width)
    return split.transpose(0, 3, 1, 2, 4).reshape(members, rows, width)


def up_kernel(ids, scaled, *refs):
    weights, before, hidden, gains = refs[:8], refs[8], refs[9], refs[10]
    rows = before.shape[0]
    total = jnp.zeros((scaled.shape[1], before.shape[1]), F32)
    for at in range(8):
        total = total + dot(scaled[ids[0] ^ at], weights[at][...], 1, 0)
    value = total[:rows]
    before[...] = value
    bend = jnp.tanh(GELU_C * (value + GELU_A * value * value * value))
    hidden[...] = (0.5 * value * (1.0 + bend)).astype(BF16)
    gains[...] = jnp.sum(total[rows:], axis=0, keepdims=True)


def down_kernel(ids, hidden, *refs):
    weights, keep, send = refs[:8], refs[8], refs[9]
    _, pairs, quarter, width = keep.shape
    for at in range(8):
        block = ids[0] ^ at
        value = dot(hidden[...], weights[at][...], 1, 1).reshape(pairs, 2, quarter, width)
        odd = ids[1] == 1
        keep[block] = jnp.where(odd, value[:, 1], value[:, 0])
        send[block] = jnp.where(odd, value[:, 0], value[:, 1]).astype(BF16)


def back_kernel(ids, near, far, before, gains, *refs):
    downs, ups, outs, first, second = refs[:8], refs[8:16], refs[16], refs[17], refs[18]
    rows, hidden = before.shape
    half = rows // 2
    total = jnp.zeros((rows, hidden), F32)
    for at in range(8):
        block = ids[0] ^ at
        width = downs[at].shape[0]
        upstream = jnp.concatenate(
            [near[:, block].reshape(half, width), far[:, block].reshape(half, width)]
        )
        total = total + dot(upstream, downs[at][...], 1, 0)
    value = before[...]
    square = value * value
    bend = jnp.tanh(GELU_C * value * (1.0 + GELU_A * square))
    slope = 0.5 * (1.0 + bend) + 0.5 * GELU_C * value * (1.0 - bend * bend) * (
        1.0 + 3.0 * GELU_A * square
    )
    grad16 = (total * slope).astype(BF16)
    grad = grad16.astype(F32)
    first[...] = jnp.sum(grad * gains[...], axis=1, keepdims=True)
    second[...] = jnp.sum(grad * value, axis=1, keepdims=True)
    for at in range(8):
        outs[ids[0] ^ at] = dot(grad16, ups[at][...], 1, 1)


def call(kernel, name, shapes, *operands):
    flops = 2 * 256 * 1792 * 960 * (2 if name == "back" else 1)
    return pl.pallas_call(
        kernel,
        out_shape=shapes,
        in_specs=[SMEM] + [VMEM] * (len(operands) - 1),
        out_specs=tuple(VMEM for _ in shapes),
        compiler_params=PARAMS,
        cost_estimate=pl.CostEstimate(flops=flops, bytes_accessed=6 << 20, transcendentals=0),
        name=name,
    )(*operands)


def norm_stats(rows, axes):
    mean = jnp.mean(rows, axis=axes, keepdims=True)
    centered = rows - mean
    return mean, lax.rsqrt(jnp.mean(centered * centered, axis=axes, keepdims=True) + EPS)


def packed(data, sums):
    high = lax.reduce_precision(sums, 8, 7)
    tail = jnp.concatenate([high, sums - high], -1).astype(BF16)
    return jnp.concatenate([data.astype(BF16), jnp.broadcast_to(tail, data.shape[:-1] + (4,))], -1)


def unpacked(payload, cols):
    payload = payload.astype(F32)
    sums = payload[0, :, cols : cols + 2] + payload[0, :, cols + 2 : cols + 4]
    return payload[..., :cols], sums


def norm_back(grad, sums, rows, mean, inverse, gain, features):
    normed = (rows - mean) * inverse
    first, second = sums[:, 0:1] / features, sums[:, 1:2] / features
    return inverse * (grad * gain - first - normed * second)


def unit_rows(embed):
    inv = lax.rsqrt(jnp.sum(embed * embed, axis=1, keepdims=True) + EPS)
    return inv, (embed * inv).astype(BF16)


def unit_back(embed, inv, grad):
    along = jnp.sum(embed * grad, axis=1, keepdims=True)
    return inv * (grad - embed * (inv * inv) * along)


def gelu16(before):
    return jax.nn.gelu(before, approximate=True).astype(BF16)


def gelu_back16(before, grad):
    _, back = jax.vjp(lambda value: jax.nn.gelu(value, approximate=True), before)
    return back(grad)[0].astype(BF16)


def shards(
    image_in,
    text_in,
    image_gain,
    text_gain,
    image_up,
    image_down,
    text_up,
    text_down,
    image_head,
    log_scale,
    bias,
):
    img, grp = lax.axis_index("img"), lax.axis_index("grp")
    x, core = grp // 2, grp % 2
    members = lax.axis_size("img")
    top = members // 2
    rows, image_cols = image_in.shape
    quarter = rows // 4
    text_cols = text_in.shape[1]
    image_features, text_features = image_cols * 4, text_cols * 4
    width = image_features // members
    share_count = members // 4
    hidden_half = image_up.shape[1] // 2
    embed_width = image_head.shape[1]
    scale = jnp.exp(log_scale[0])
    shift = bias[0]
    ids = jnp.stack([img // top * 4 + img % 4, core]).astype(jnp.int32)

    with jax.named_scope("weights"):
        near_up, far_up = halves(image_up, img)
        far_up = swap(far_up, "img", top)
        near_down, far_down = halves(image_down.T, img)
        far_down = swap(far_down, "img", top)
        ups, downs = [], []
        for near, far in ((near_up, far_up), (near_down, far_down)):
            groups = []
            for block in (near, far):
                block = widen(block, img)
                by_two = swap(block, "img", 2)
                groups += [block, swap(block, "img", 1), by_two, swap(by_two, "img", 1)]
            (downs if ups else ups).extend(groups)

    with jax.named_scope("image_rows"):
        own_in = image_in.reshape(rows, share_count, width).transpose(1, 0, 2)
        both = jnp.stack([own_in, swap(own_in, "img", top)], 1)
        both = jnp.stack([both, swap(both, "grp", 2)])
        both = jnp.concatenate([both, swap(both, "grp", 1)])
        whole = place([both[at] for at in range(4)], grp, FLIPS)
        whole = whole.reshape(members, 2 * rows, width)
        whole32 = whole.astype(F32)
        mean, inverse = norm_stats(whole32, (0, 2))
        gain = image_gain.reshape(members, 1, width)
        scaled = ((whole32 - mean) * inverse * gain).astype(BF16)
        parts, rest = [], gain
        for _ in range(3):
            part = lax.reduce_precision(rest, 8, 7)
            parts.append(part.astype(BF16))
            rest = rest - part
        parts.append(jnp.zeros((members, 13, width), BF16))
        scaled = blocked(jnp.concatenate([scaled] + parts, 1))

    with jax.named_scope("text_forward"):
        pair = jnp.stack([text_in, swap(text_in, "grp", 2)])
        parts = jnp.concatenate([pair, swap(pair, "grp", 1)])
        parts = place([parts[at] for at in range(4)], grp, FLIPS)
        text_whole = parts.transpose(1, 0, 2).reshape(rows, text_features).astype(F32)
        text_mean, text_inverse = norm_stats(text_whole, 1)
        text_normed = (text_whole - text_mean) * text_inverse
        text_before = dot((text_normed * text_gain).astype(BF16), text_up, 1, 0)
        text_branch = dot(gelu16(text_before), text_down, 1, 0)
        text_branch = text_branch.reshape(2, 2, quarter, text_features)
        send = take(text_branch, 1 - core, 1).astype(BF16)
        total = take(text_branch, core, 1) + swap(send, "grp", 1).astype(F32)
        send = take(total, 1 - x).astype(BF16)
        total = take(total, x) + swap(send, "grp", 2).astype(F32)
        text_embed = lax.dynamic_slice_in_dim(text_whole, grp * quarter, quarter, 0) + total
        text_inv, text_unit = unit_rows(text_embed)
        text_gains = jnp.sum(text_up.astype(F32) * text_gain[:, None], axis=0)

    with jax.named_scope("text_units"):
        held, flips, bit = text_unit[None], [0], 1
        while bit < members:
            held = jnp.concatenate([held, swap(held, "img", bit)])
            flips = flips + [flip ^ bit for flip in flips]
            bit *= 2
        share = place([held[at] for at in range(members)], img, flips)
        share = share.reshape(members * quarter, embed_width)
        pair = jnp.stack([share, swap(share, "grp", 2)])
        every = jnp.concatenate([pair, swap(pair, "grp", 1)])
        every_text = every.reshape(4 * members * quarter, embed_width)
        at = jnp.arange(members * quarter, dtype=jnp.int32)
        share_ids = at // quarter * rows + at % quarter
        text_ids = jnp.concatenate([share_ids + (grp ^ flip) * quarter for flip in FLIPS])

    with jax.named_scope("head"):
        pair = jnp.stack([image_head, swap(image_head, "grp", 2)])
        pairs = jnp.concatenate([pair, swap(pair, "grp", 1)])
        head = place([pairs[at] for at in range(4)], grp, FLIPS)
        head = head.reshape(members, width, embed_width)

    with jax.named_scope("image_forward"):
        before, hidden, gains = call(
            up_kernel,
            "up",
            (
                jax.ShapeDtypeStruct((2 * rows, hidden_half), F32),
                jax.ShapeDtypeStruct((2 * rows, hidden_half), BF16),
                jax.ShapeDtypeStruct((1, hidden_half), F32),
            ),
            ids,
            scaled,
            *ups,
        )
        shape = (8, 4, quarter, image_features // 8)
        keep, send = call(
            down_kernel,
            "down",
            (jax.ShapeDtypeStruct(shape, F32), jax.ShapeDtypeStruct(shape, BF16)),
            ids,
            hidden,
            *downs,
        )
        total = (keep + swap(send, "grp", 1).astype(F32)).reshape(8, 2, 2, quarter, -1)
        send = take(total, 1 - x, 2).astype(BF16)
        total = take(total, x, 2) + swap(send, "grp", 2).astype(F32)
        branch = total[:, 0] + swap(total[:, 1].astype(BF16), "img", top).astype(F32)
        own_rows = lax.dynamic_slice_in_dim(whole, grp * quarter, quarter, 1).astype(F32)
        image_mid16 = (own_rows + in_order(branch, members)).astype(BF16)
        image_mid16 = image_mid16.transpose(1, 0, 2).reshape(quarter, image_features)
        image_embed = dot(image_mid16, head.reshape(image_features, embed_width), 1, 0)
        image_inv, image_unit = unit_rows(image_embed)

    with jax.named_scope("image_loss"):
        image_ids = img * rows + grp * quarter + jnp.arange(quarter, dtype=jnp.int32)
        logits = scale * dot(image_unit, every_text, 1, 1) + shift
        same = (image_ids[:, None] == text_ids[None, :]).astype(F32)
        pull = (jax.nn.sigmoid(logits) - same).astype(BF16)
        grad_image_unit = scale * dot(pull, every_text, 1, 0)
        grad_embed16 = unit_back(image_embed, image_inv, grad_image_unit).astype(BF16)
        grad_mid16 = dot(grad_embed16, head.reshape(image_features, embed_width), 1, 1)
        grad_mid16 = grad_mid16.astype(BF16).reshape(quarter, members, width)
        grad_mid16 = blocked(grad_mid16.transpose(1, 0, 2))

    with jax.named_scope("image_backward"):
        far_grad = swap(grad_mid16, "img", top)
        near_whole = lax.all_gather(grad_mid16, "grp")
        far_whole = lax.all_gather(far_grad, "grp")
        partial, first, second = call(
            back_kernel,
            "back",
            (
                jax.ShapeDtypeStruct((8, 2 * rows, image_features // 8), F32),
                jax.ShapeDtypeStruct((2 * rows, 1), F32),
                jax.ShapeDtypeStruct((2 * rows, 1), F32),
            ),
            ids,
            near_whole,
            far_whole,
            before,
            gains,
            *downs,
            *ups,
        )
        sums = jnp.concatenate([first, second], 1)
        partial = in_order(partial, members).reshape(2, 2, share_count, 2 * rows, width)
        send = packed(take(partial, 1 - core, 1), sums)
        got = swap(send, "grp", 1).reshape(2 * share_count, 2 * rows, width + 4)
        data, more = unpacked(got, width)
        total = take(partial, core, 1) + data.reshape(2, share_count, 2 * rows, width)
        sums = sums + more
        data, more = unpacked(swap(packed(take(total, 1 - x), sums), "grp", 2), width)
        total, sums = take(total, x) + data, sums + more
        send = packed(total[:, rows:], sums[rows:])
        data, more = unpacked(swap(send, "img", top), width)
        total, sums = total[:, :rows] + data, sums[:rows] + more
        back = norm_back(
            total,
            sums,
            own_in.astype(F32),
            mean[0, :rows],
            inverse[0, :rows],
            take(gain.reshape(4, share_count, 1, width), grp),
            image_features,
        )
        own_grad = in_order(near_whole.transpose(1, 0, 2, 3).reshape(8, rows, -1), members)
        own_grad = take(own_grad.reshape(4, share_count, rows, width), grp)
        image_grad = (own_grad.astype(F32) + back).astype(BF16)
        image_grad = image_grad.transpose(1, 0, 2).reshape(rows, image_cols)

    with jax.named_scope("text_loss"):
        pair = jnp.stack([image_unit, swap(image_unit, "grp", 2)])
        image_units = jnp.concatenate([pair, swap(pair, "grp", 1)]).reshape(rows, embed_width)
        logits = scale * dot(image_units, share, 1, 1) + shift
        at = jnp.arange(quarter, dtype=jnp.int32)
        group_ids = jnp.concatenate([img * rows + (grp ^ flip) * quarter + at for flip in FLIPS])
        same = (group_ids[:, None] == (share_ids + grp * quarter)[None, :]).astype(F32)
        pull = (jax.nn.sigmoid(logits) - same).astype(BF16)
        partial = (scale * dot(pull, image_units, 0, 0)).astype(BF16)
        partial = partial.reshape(members, quarter, embed_width)
        parts = lax.all_to_all(partial, "img", split_axis=0, concat_axis=0, tiled=True)
        grad_text_unit = jnp.sum(parts.astype(F32), axis=0)
        grad_text16 = unit_back(text_embed, text_inv, grad_text_unit).astype(BF16)

    with jax.named_scope("text_backward"):
        pair = jnp.stack([grad_text16, swap(grad_text16, "grp", 2)])
        parts = jnp.concatenate([pair, swap(pair, "grp", 1)])
        upstream = place([parts[at] for at in range(4)], grp, FLIPS).reshape(rows, text_features)
        grad_before = gelu_back16(text_before, dot(upstream, text_down, 1, 1))
        grad32 = grad_before.astype(F32)
        sums = jnp.stack([jnp.sum(grad32 * text_gains, 1), jnp.sum(grad32 * text_before, 1)], 1)
        blocks = text_up.reshape(4, text_cols, -1)
        partial = {flip: dot(grad_before, take(blocks, grp ^ flip), 1, 1) for flip in FLIPS}
        send = jnp.stack([packed(partial[flip], sums) for flip in (1, 3)])
        data, more = unpacked(swap(send, "grp", 1), text_cols)
        sums = sums + more
        send = packed(partial[2] + data[1], sums)[None]
        more_data, more = unpacked(swap(send, "grp", 2), text_cols)
        total, sums = partial[0] + data[0] + more_data[0], sums + more
        own_gain = lax.dynamic_slice_in_dim(text_gain, grp * text_cols, text_cols, 0)
        back = norm_back(
            total, sums, text_in.astype(F32), text_mean, text_inverse, own_gain, text_features
        )
        own_grad = lax.dynamic_slice_in_dim(upstream, grp * text_cols, text_cols, 1)
        text_grad = (own_grad.astype(F32) + back).astype(BF16)
    return (image_grad, text_grad)


def solution(mesh):
    in_specs = (
        P("img", "grp"),
        P("img", "grp"),
        P(),
        P(),
        P("img", "grp"),
        P("grp", "img"),
        P(None, "grp"),
        P("grp", None),
        P("grp", None),
        P(),
        P(),
    )
    out_specs = (P("img", "grp"), P("img", "grp"))
    return jax.shard_map(shards, mesh=mesh, in_specs=in_specs, out_specs=out_specs, check_vma=False)
```

```python
import functools

import jax
import jax.numpy as jnp
from jax import lax
from jax.experimental import pallas as pl
from jax.experimental.pallas import tpu as pltpu
from jax.sharding import PartitionSpec as P

EPS = 1e-06
BF16 = jnp.bfloat16
F32 = jnp.float32
FLIPS = (0, 2, 1, 3)
GELU_C = 0.7978845608028654
GELU_A = 0.044715
VMEM = pl.BlockSpec(memory_space=pltpu.VMEM)
SMEM = pl.BlockSpec(memory_space=pltpu.SMEM)
ANY = pl.BlockSpec(memory_space=pl.ANY)
TAIL = 32
PARAMS = pltpu.CompilerParams(vmem_limit_bytes=60 * 1024 * 1024)


def swap(value, axis, flip):
    return lax.ppermute(value, axis, [(i, i ^ flip) for i in range(lax.axis_size(axis))])


def place(parts, index, flips):
    whole = jnp.zeros((len(flips),) + parts[0].shape, parts[0].dtype)
    for part, flip in zip(parts, flips):
        whole = lax.dynamic_update_index_in_dim(whole, part, index ^ flip, 0)
    return whole


def tie(value, *events):
    return lax.optimization_barrier((value,) + events)[0]


def dot(left, right, left_dim, right_dim):
    dims = (((left_dim,), (right_dim,)), ((), ()))
    return lax.dot_general(left, right, dims, preferred_element_type=F32)


def take(array, index, axis=0):
    return lax.dynamic_index_in_dim(array, index, axis, False)


def halves(shard, img):
    half = shard.shape[-1] // 2
    low, high = shard[..., :half], shard[..., half:]
    upper = img >= lax.axis_size("img") // 2
    return jnp.where(upper, high, low), jnp.where(upper, low, high)


def widen(block, img):
    members = lax.axis_size("img")
    held, flips, bit = block[None], [0], 4
    while bit < members // 2:
        held = jnp.concatenate([held, swap(held, "img", bit)])
        flips = flips + [flip ^ (bit // 4) for flip in flips]
        bit *= 2
    if len(flips) == 1:
        return block
    middle = img // 4 % (members // 8)
    held = place([held[at] for at in range(len(flips))], middle, flips)
    return held.transpose(1, 0, 2, 3).reshape(2, -1, block.shape[2])


def blocked(natural):
    members, rows, width = natural.shape
    if members == 8:
        return natural
    split = natural.reshape(2, members // 8, 4, rows, width)
    return split.transpose(0, 2, 3, 1, 4).reshape(8, rows, members // 8 * width)


def in_order(blocks, members):
    if members == 8:
        return blocks
    rows, width = blocks.shape[1], blocks.shape[2] * 8 // members
    split = blocks.reshape(2, 4, rows, members // 8, width)
    return split.transpose(0, 3, 1, 2, 4).reshape(members, rows, width)


def norm_kernel(ids, parts, gain, scaled, own, mean, inverse):
    _, share_count, rows, _ = parts.shape
    quarter = own.shape[1]
    features = float(4 * share_count * parts.shape[3])
    picks = [(at, sub) for at in range(4) for sub in range(share_count)]

    def sum_rows(term):
        return sum(jnp.sum(term(parts[pick].astype(F32)), axis=1, keepdims=True) for pick in picks)

    center = sum_rows(lambda value: value) / features
    variance = sum_rows(lambda value: (value - center) * (value - center)) / features
    factor = lax.rsqrt(variance + EPS)
    mean[...] = center
    inverse[...] = factor
    start = pl.multiple_of(ids[2] * quarter, quarter)
    for at, sub in picks:
        block = (ids[2] ^ FLIPS[at]) * share_count + sub
        value = parts[at, sub].astype(F32)
        scaled[block, :rows] = ((value - center) * factor * gain[block]).astype(BF16)
        own[block] = parts[at, sub, pl.ds(start, quarter)]
        rest = jnp.broadcast_to(gain[block], (16, gain.shape[2]))
        line = lax.broadcasted_iota(jnp.int32, rest.shape, 0)
        split = jnp.zeros_like(rest)
        for index in range(3):
            part = rest.astype(BF16).astype(F32)
            split = jnp.where(line == index, part, split)
            rest = rest - part
        scaled[block, rows:] = split.astype(BF16)


def fetch(which, blocks, buffer, sems):
    copies = []
    for at, block in enumerate(blocks):
        source, slot = block.at[which] if at < 7 else block, which * 8 + at
        copies.append(pltpu.make_async_copy(source, buffer.at[slot], sems.at[slot]))
    for copy in copies:
        copy.start()
    return copies


def forward_kernel(ids, scaled, *refs):
    before, gains, keep, send, buffer, sems = refs[9:]
    ups = fetch(0, refs[:8], buffer, sems)
    downs = fetch(1, refs[:7] + refs[8:9], buffer, sems)
    rows = before.shape[0]
    total = jnp.zeros((scaled.shape[1], before.shape[1]), F32)
    for at in range(8):
        ups[at].wait()
        total = total + dot(scaled[ids[0] ^ at], buffer[at], 1, 0)
    value = total[:rows]
    before[...] = value
    bend = jnp.tanh(GELU_C * (value + GELU_A * value * value * value))
    hidden = (0.5 * value * (1.0 + bend)).astype(BF16)
    gains[...] = jnp.sum(total[rows:], axis=0, keepdims=True)
    _, pairs, quarter, width = keep.shape
    for at in range(8):
        downs[at].wait()
        block = ids[0] ^ at
        value = dot(hidden, buffer[8 + at], 1, 1).reshape(pairs, 2, quarter, width)
        odd = ids[1] == 1
        keep[block] = jnp.where(odd, value[:, 1], value[:, 0])
        send[block] = jnp.where(odd, value[:, 0], value[:, 1]).astype(BF16)


def back_kernel(split, ids, near, far, before, gains, *refs):
    outs, others, buffer, sems = refs[9:]
    downs = fetch(1, refs[:7] + refs[8:9], buffer, sems)
    ups = fetch(0, refs[:8], buffer, sems)
    rows, hidden = before.shape
    half, width = rows // 2, buffer.shape[1]
    total = jnp.zeros((rows, hidden), F32)
    for at in range(8):
        downs[at].wait()
        block = ids[0] ^ at
        upstream = jnp.concatenate(
            [near[:, block].reshape(half, width), far[:, block].reshape(half, width)]
        )
        total = total + dot(upstream, buffer[8 + at], 1, 0)
    value = before[...]
    square = value * value
    bend = jnp.tanh(GELU_C * value * (1.0 + GELU_A * square))
    slope = 0.5 * (1.0 + bend) + 0.5 * GELU_C * value * (1.0 - bend * bend) * (
        1.0 + 3.0 * GELU_A * square
    )
    grad16 = (total * slope).astype(BF16)
    grad = grad16.astype(F32)
    first = jnp.sum(grad * gains[...], axis=1, keepdims=True)
    second = jnp.sum(grad * value, axis=1, keepdims=True)
    lane = lax.broadcasted_iota(jnp.int32, (rows, TAIL), 1)
    tail = jnp.where(lane == 0, first, jnp.where(lane == 1, second, 0.0))
    for copy in ups:
        copy.wait()
    if not split:
        others[...] = tail
        for at in range(8):
            outs[ids[0] ^ at] = dot(grad16, buffer[at], 1, 1)
        return
    for ref, core in ((others, 1 - ids[1]), (outs, ids[1])):
        for at in range(4):
            block = at // 2 * 4 + core * 2 + at % 2
            value = dot(grad16, buffer[ids[0] ^ block], 1, 1)
            ref[at // 2, at % 2, :, :width] = value.astype(ref.dtype)
            ref[at // 2, at % 2, :, width:] = tail.astype(ref.dtype)


def call(kernel, name, shapes, operands, weights=()):
    scratch = []
    if weights:
        scratch.append(pltpu.VMEM((16,) + weights[0].shape[1:], BF16))
        scratch.append(pltpu.SemaphoreType.DMA((16,)))
    flops = 2 * 256 * 224 * 960 * 16 if weights else 0
    return pl.pallas_call(
        kernel,
        out_shape=shapes,
        in_specs=[SMEM] + [VMEM] * (len(operands) - 1) + [ANY] * len(weights),
        out_specs=tuple(VMEM for _ in shapes),
        scratch_shapes=scratch,
        compiler_params=PARAMS,
        cost_estimate=pl.CostEstimate(flops=flops, bytes_accessed=6 << 20, transcendentals=0),
        name=name,
    )(*operands, *weights)


def norm_stats(rows, axes):
    mean = jnp.mean(rows, axis=axes, keepdims=True)
    centered = rows - mean
    return mean, lax.rsqrt(jnp.mean(centered * centered, axis=axes, keepdims=True) + EPS)


def packed(data, sums):
    high = lax.reduce_precision(sums, 8, 7)
    tail = jnp.concatenate([high, sums - high], -1).astype(BF16)
    return jnp.concatenate([data.astype(BF16), jnp.broadcast_to(tail, data.shape[:-1] + (4,))], -1)


def unpacked(payload, cols):
    payload = payload.astype(F32)
    sums = payload[0, :, cols : cols + 2] + payload[0, :, cols + 2 : cols + 4]
    return payload[..., :cols], sums


def norm_back(grad, sums, rows, mean, inverse, gain, features):
    normed = (rows - mean) * inverse
    first, second = sums[:, 0:1] / features, sums[:, 1:2] / features
    return inverse * (grad * gain - first - normed * second)


def unit_rows(embed):
    inv = lax.rsqrt(jnp.sum(embed * embed, axis=1, keepdims=True) + EPS)
    return inv, (embed * inv).astype(BF16)


def unit_back(embed, inv, grad):
    along = jnp.sum(embed * grad, axis=1, keepdims=True)
    return inv * (grad - embed * (inv * inv) * along)


def gelu16(before):
    return jax.nn.gelu(before, approximate=True).astype(BF16)


def gelu_back16(before, grad):
    _, back = jax.vjp(lambda value: jax.nn.gelu(value, approximate=True), before)
    return back(grad)[0].astype(BF16)


def shards(
    image_in,
    text_in,
    image_gain,
    text_gain,
    image_up,
    image_down,
    text_up,
    text_down,
    image_head,
    log_scale,
    bias,
):
    img, grp = lax.axis_index("img"), lax.axis_index("grp")
    x, core = grp // 2, grp % 2
    members = lax.axis_size("img")
    top = members // 2
    rows, image_cols = image_in.shape
    quarter = rows // 4
    text_cols = text_in.shape[1]
    image_features, text_features = image_cols * 4, text_cols * 4
    width = image_features // members
    share_count = members // 4
    hidden_half = image_up.shape[1] // 2
    embed_width = image_head.shape[1]
    scale = jnp.exp(log_scale[0])
    shift = bias[0]
    ids = jnp.stack([img // top * 4 + img % 4, core, grp]).astype(jnp.int32)

    gate = lax.optimization_barrier

    with jax.named_scope("first"):
        near, send = halves(jnp.stack([image_up, image_down.T]), img)
        near, far = widen(near, img), widen(swap(send, "img", top), img)
        near_y, near_z = swap(near, "img", 1), swap(near, "img", 2)
        near_zy = swap(near_z, "img", 1)
        text_x = swap(text_in, "grp", 2)
        text_parts = [text_in, text_x, swap(text_in, "grp", 1), swap(text_x, "grp", 1)]
        text_parts = place(text_parts, grp, FLIPS)
        text_whole = text_parts.transpose(1, 0, 2).reshape(rows, text_features).astype(F32)
        text_mean, text_inverse = norm_stats(text_whole, 1)
        text_normed = (text_whole - text_mean) * text_inverse
        text_before = dot((text_normed * text_gain).astype(BF16), text_up, 1, 0)
        text_branch = dot(gelu16(text_before), text_down, 1, 0)
        text_branch = text_branch.reshape(2, 2, quarter, text_features)
        send = take(text_branch, 1 - core, 1).astype(BF16)
        total = take(text_branch, core, 1) + swap(send, "grp", 1).astype(F32)
        send = take(total, 1 - x).astype(BF16)
        total = take(total, x) + swap(send, "grp", 2).astype(F32)
        own_in = image_in.reshape(rows, share_count, width).transpose(1, 0, 2)
        far_in = swap(own_in, "img", top)
        head_x = swap(tie(image_head, text_parts), "grp", 2)
        far, near_y, near_zy, total, far_in, head_x = gate(
            (far, near_y, near_zy, total, far_in, head_x)
        )

    with jax.named_scope("second"):
        far_y, far_z = swap(far, "img", 1), swap(far, "img", 2)
        both = jnp.concatenate([own_in, far_in], 1)
        both = jnp.stack([both, swap(both, "grp", 2)])
        text_embed = lax.dynamic_slice_in_dim(text_whole, grp * quarter, quarter, 0) + total
        text_inv, text_unit = unit_rows(text_embed)
        copies = jnp.broadcast_to(text_unit, (members,) + text_unit.shape)
        share = lax.all_to_all(copies, "img", split_axis=0, concat_axis=0, tiled=True)
        far_y, far_z, both, share = gate((far_y, far_z, both, share))

    with jax.named_scope("third"):
        up_last, down_last = swap(far_z[0], "img", 1), swap(far_y[1], "img", 2)
        weights = [near, near_y, near_z, near_zy, far, far_y, far_z, up_last, down_last]
        both = jnp.concatenate([both, swap(both, "grp", 1)])
        text_gains = jnp.sum(text_up.astype(F32) * text_gain[:, None], axis=0)
        share = share.reshape(members * quarter, embed_width)
        at = jnp.arange(members * quarter, dtype=jnp.int32)
        share_ids = at // quarter * rows + at % quarter
        text_ids = jnp.concatenate([share_ids + (grp ^ flip) * quarter for flip in FLIPS])

    with jax.named_scope("norm"):
        share_x = swap(share, "grp", 2)
        every = [share, share_x, swap(share, "grp", 1), swap(share_x, "grp", 1)]
        every_text = jnp.concatenate(every)
        heads = [image_head, head_x, swap(image_head, "grp", 1), swap(head_x, "grp", 1)]
        head = place(heads, grp, FLIPS).reshape(members, width, embed_width)
        gain = image_gain.reshape(members, 1, width)
        scaled, own_rows, mean, inverse = call(
            norm_kernel,
            "norm",
            (
                jax.ShapeDtypeStruct((members, 2 * rows + 16, width), BF16),
                jax.ShapeDtypeStruct((members, quarter, width), BF16),
                jax.ShapeDtypeStruct((2 * rows, 1), F32),
                jax.ShapeDtypeStruct((2 * rows, 1), F32),
            ),
            (ids, both, gain),
        )
        scaled = blocked(tie(scaled, share_x, head))

    with jax.named_scope("image_forward"):
        shape = (8, 4, quarter, image_features // 8)
        before, gains, keep, send = call(
            forward_kernel,
            "forward",
            (
                jax.ShapeDtypeStruct((2 * rows, hidden_half), F32),
                jax.ShapeDtypeStruct((1, hidden_half), F32),
                jax.ShapeDtypeStruct(shape, F32),
                jax.ShapeDtypeStruct(shape, BF16),
            ),
            (ids, scaled),
            weights,
        )
        total = (keep + swap(send, "grp", 1).astype(F32)).reshape(8, 2, 2, quarter, -1)
        send = take(total, 1 - x, 2).astype(BF16)
        got = swap(send, "grp", 2)
        total = take(total, x, 2) + got.astype(F32)
        branch = total[:, 0] + swap(total[:, 1].astype(BF16), "img", top).astype(F32)
        image_mid16 = (own_rows.astype(F32) + in_order(branch, members)).astype(BF16)
        image_mid16 = image_mid16.transpose(1, 0, 2).reshape(quarter, image_features)
        image_embed = dot(image_mid16, head.reshape(image_features, embed_width), 1, 0)
        image_inv, image_unit = unit_rows(image_embed)

    with jax.named_scope("text_loss"):
        pair = jnp.stack([image_unit, swap(image_unit, "grp", 2)])
        image_units = jnp.concatenate([pair, swap(pair, "grp", 1)]).reshape(rows, embed_width)
        logits = scale * dot(image_units, share, 1, 1) + shift
        at = jnp.arange(quarter, dtype=jnp.int32)
        group_ids = jnp.concatenate([img * rows + (grp ^ flip) * quarter + at for flip in FLIPS])
        same = (group_ids[:, None] == (share_ids + grp * quarter)[None, :]).astype(F32)
        pull = (jax.nn.sigmoid(logits) - same).astype(BF16)
        text_partial = (scale * dot(pull, image_units, 0, 0)).astype(BF16)
        text_partial = text_partial.reshape(members, quarter, embed_width)
        text_parts = lax.all_to_all(
            text_partial, "img", split_axis=0, concat_axis=0, tiled=True
        )

    with jax.named_scope("image_loss"):
        image_ids = img * rows + grp * quarter + jnp.arange(quarter, dtype=jnp.int32)
        logits = scale * dot(image_unit, every_text, 1, 1) + shift
        same = (image_ids[:, None] == text_ids[None, :]).astype(F32)
        pull = (jax.nn.sigmoid(logits) - same).astype(BF16)
        grad_image_unit = scale * dot(pull, every_text, 1, 0)
        grad_embed16 = unit_back(image_embed, image_inv, grad_image_unit).astype(BF16)
        grad_mid16 = dot(grad_embed16, head.reshape(image_features, embed_width), 1, 1)
        grad_mid16 = grad_mid16.astype(BF16).reshape(quarter, members, width)
        grad_mid16 = blocked(grad_mid16.transpose(1, 0, 2))

    with jax.named_scope("image_backward"):
        far_grad = swap(grad_mid16, "img", top)
        near_whole = lax.all_gather(grad_mid16, "grp")
        far_whole = lax.all_gather(tie(far_grad, text_partial), "grp")
        split = members == 8
        if split:
            shape = (2, share_count, 2 * rows, width + TAIL)
            shapes = (jax.ShapeDtypeStruct(shape, F32), jax.ShapeDtypeStruct(shape, BF16))
        else:
            shapes = (
                jax.ShapeDtypeStruct((8, 2 * rows, image_features // 8), F32),
                jax.ShapeDtypeStruct((2 * rows, TAIL), F32),
            )
        keep, send = call(
            functools.partial(back_kernel, split),
            "back",
            shapes,
            (ids, near_whole, far_whole, before, gains),
            weights,
        )
        if not split:
            tail = jnp.broadcast_to(send, (members,) + send.shape)
            total = jnp.concatenate([in_order(keep, members), tail], -1)
            total = total.reshape(2, 2, share_count, 2 * rows, width + TAIL)
            keep, send = take(total, core, 1), take(total, 1 - core, 1).astype(BF16)
        total = keep + tie(swap(send, "grp", 1), text_parts).astype(F32)
        send = take(total, 1 - x).astype(BF16)
        total = take(total, x) + swap(send, "grp", 2).astype(F32)
        got = swap(total[:, rows:].astype(BF16), "img", top).astype(F32)
        total = total[:, :rows] + got
        total, sums = total[..., :width], total[0, :, width : width + 2]
        back = norm_back(
            total,
            sums,
            own_in.astype(F32),
            mean[:rows],
            inverse[:rows],
            take(gain.reshape(4, share_count, 1, width), grp),
            image_features,
        )
        own_grad = in_order(near_whole.transpose(1, 0, 2, 3).reshape(8, rows, -1), members)
        own_grad = take(own_grad.reshape(4, share_count, rows, width), grp)
        image_grad = (own_grad.astype(F32) + back).astype(BF16)
        image_grad = image_grad.transpose(1, 0, 2).reshape(rows, image_cols)

    with jax.named_scope("text_sum"):
        grad_text_unit = jnp.sum(text_parts.astype(F32), axis=0)
        grad_text16 = unit_back(text_embed, text_inv, grad_text_unit).astype(BF16)

    with jax.named_scope("text_backward"):
        pair = jnp.stack([grad_text16, swap(grad_text16, "grp", 2)])
        parts = jnp.concatenate([pair, swap(pair, "grp", 1)])
        upstream = place([parts[at] for at in range(4)], grp, FLIPS).reshape(rows, text_features)
        grad_before = gelu_back16(text_before, dot(upstream, text_down, 1, 1))
        grad32 = grad_before.astype(F32)
        sums = jnp.stack([jnp.sum(grad32 * text_gains, 1), jnp.sum(grad32 * text_before, 1)], 1)
        blocks = text_up.reshape(4, text_cols, -1)
        partial = {flip: dot(grad_before, take(blocks, grp ^ flip), 1, 1) for flip in FLIPS}
        send = jnp.stack([packed(partial[flip], sums) for flip in (1, 3)])
        data, more = unpacked(swap(send, "grp", 1), text_cols)
        sums = sums + more
        send = packed(partial[2] + data[1], sums)[None]
        more_data, more = unpacked(swap(send, "grp", 2), text_cols)
        total, sums = partial[0] + data[0] + more_data[0], sums + more
        own_gain = lax.dynamic_slice_in_dim(text_gain, grp * text_cols, text_cols, 0)
        back = norm_back(
            total, sums, text_in.astype(F32), text_mean, text_inverse, own_gain, text_features
        )
        own_grad = lax.dynamic_slice_in_dim(upstream, grp * text_cols, text_cols, 1)
        text_grad = (own_grad.astype(F32) + back).astype(BF16)
    return (image_grad, text_grad)


def solution(mesh):
    in_specs = (
        P("img", "grp"),
        P("img", "grp"),
        P(),
        P(),
        P("img", "grp"),
        P("grp", "img"),
        P(None, "grp"),
        P("grp", None),
        P("grp", None),
        P(),
        P(),
    )
    out_specs = (P("img", "grp"), P("img", "grp"))
    return jax.shard_map(shards, mesh=mesh, in_specs=in_specs, out_specs=out_specs, check_vma=False)
```

```python
import functools

import jax
import jax.numpy as jnp
from jax import lax
from jax.experimental import pallas as pl
from jax.experimental.pallas import tpu as pltpu
from jax.sharding import PartitionSpec as P

EPS = 1e-06
BF16 = jnp.bfloat16
F32 = jnp.float32
FLIPS = (0, 2, 1, 3)
GELU_C = 0.7978845608028654
GELU_A = 0.044715
VMEM = pl.BlockSpec(memory_space=pltpu.VMEM)
SMEM = pl.BlockSpec(memory_space=pltpu.SMEM)
ANY = pl.BlockSpec(memory_space=pl.ANY)
TAIL = 32
SLOTS = (0, 1, 2, 4, 3, 5, 6, 7)
PAIRED = 5
PARAMS = pltpu.CompilerParams(vmem_limit_bytes=60 * 1024 * 1024)


def swap(value, axis, flip):
    return lax.ppermute(value, axis, [(i, i ^ flip) for i in range(lax.axis_size(axis))])


def place(parts, index, flips):
    whole = jnp.zeros((len(flips),) + parts[0].shape, parts[0].dtype)
    for part, flip in zip(parts, flips):
        whole = lax.dynamic_update_index_in_dim(whole, part, index ^ flip, 0)
    return whole


def tie(value, *events):
    return lax.optimization_barrier((value,) + events)[0]


def dot(left, right, left_dim, right_dim):
    dims = (((left_dim,), (right_dim,)), ((), ()))
    return lax.dot_general(left, right, dims, preferred_element_type=F32)


def take(array, index, axis=0):
    return lax.dynamic_index_in_dim(array, index, axis, False)


def exchange(halves, img):
    top = lax.axis_size("img") // 2
    pairs = [[at, at + top] for at in range(top)]
    got = lax.all_to_all(
        halves, "img", split_axis=0, concat_axis=0, tiled=True, axis_index_groups=pairs
    )
    return take(got, 1 - img // top)


def widen(block, img):
    members = lax.axis_size("img")
    held, flips, bit = block[None], [0], 4
    while bit < members // 2:
        held = jnp.concatenate([held, swap(held, "img", bit)])
        flips = flips + [flip ^ (bit // 4) for flip in flips]
        bit *= 2
    if len(flips) == 1:
        return block
    middle = img // 4 % (members // 8)
    held = place([held[at] for at in range(len(flips))], middle, flips)
    return held.transpose(1, 0, 2, 3).reshape(2, -1, block.shape[2])


def blocked(natural):
    members, rows, width = natural.shape
    if members == 8:
        return natural
    split = natural.reshape(2, members // 8, 4, rows, width)
    return split.transpose(0, 2, 3, 1, 4).reshape(8, rows, members // 8 * width)


def in_order(blocks, members):
    if members == 8:
        return blocks
    rows, width = blocks.shape[1], blocks.shape[2] * 8 // members
    split = blocks.reshape(2, 4, rows, members // 8, width)
    return split.transpose(0, 3, 1, 2, 4).reshape(members, rows, width)


def norm_kernel(ids, parts, gain, scaled, own, mean, inverse):
    _, share_count, rows, _ = parts.shape
    quarter = own.shape[1]
    features = float(4 * share_count * parts.shape[3])
    picks = [(at, sub) for at in range(4) for sub in range(share_count)]

    def sum_rows(term):
        return sum(jnp.sum(term(parts[pick].astype(F32)), axis=1, keepdims=True) for pick in picks)

    center = sum_rows(lambda value: value) / features
    variance = sum_rows(lambda value: (value - center) * (value - center)) / features
    factor = lax.rsqrt(variance + EPS)
    mean[...] = center
    inverse[...] = factor
    start = pl.multiple_of(ids[2] * quarter, quarter)
    for at, sub in picks:
        block = (ids[2] ^ FLIPS[at]) * share_count + sub
        value = parts[at, sub].astype(F32)
        scaled[block, :rows] = ((value - center) * factor * gain[block]).astype(BF16)
        own[block] = parts[at, sub, pl.ds(start, quarter)]
        rest = jnp.broadcast_to(gain[block], (16, gain.shape[2]))
        line = lax.broadcasted_iota(jnp.int32, rest.shape, 0)
        split = jnp.zeros_like(rest)
        for index in range(3):
            part = rest.astype(BF16).astype(F32)
            split = jnp.where(line == index, part, split)
            rest = rest - part
        scaled[block, rows:] = split.astype(BF16)


def fetch(which, blocks, buffer, sems):
    copies = []
    for at, block in zip(SLOTS, blocks[:5] + blocks[5 + 3 * which : 8 + 3 * which]):
        source, slot = block.at[which] if at in SLOTS[:PAIRED] else block, which * 8 + at
        copies.append((at, pltpu.make_async_copy(source, buffer.at[slot], sems.at[slot])))
    return dict(copies)


def up_kernel(ids, scaled, *refs):
    partial, buffer, sems = refs[11:]
    ups = fetch(0, refs[:11], buffer, sems)
    for at in range(7):
        ups[at].start()
    total = jnp.zeros(partial.shape, F32)
    for at in range(7):
        ups[at].wait()
        total = total + dot(scaled[ids[0] ^ at], buffer[at], 1, 0)
    partial[...] = total


def forward_kernel(ids, scaled, partial, *refs):
    before, gains, keep, send, buffer, sems = refs[11:]
    ups = fetch(0, refs[:11], buffer, sems)
    downs = fetch(1, refs[:11], buffer, sems)
    ups[7].start()
    for copy in downs.values():
        copy.start()
    rows = before.shape[0]
    ups[7].wait()
    total = partial[...] + dot(scaled[ids[0] ^ 7], buffer[7], 1, 0)
    value = total[:rows]
    before[...] = value
    bend = jnp.tanh(GELU_C * (value + GELU_A * value * value * value))
    hidden = (0.5 * value * (1.0 + bend)).astype(BF16)
    gains[...] = jnp.sum(total[rows:], axis=0, keepdims=True)
    _, pairs, quarter, width = keep.shape
    for at in range(8):
        downs[at].wait()
        block = ids[0] ^ at
        value = dot(hidden, buffer[8 + at], 1, 1).reshape(pairs, 2, quarter, width)
        odd = ids[1] == 1
        keep[block] = jnp.where(odd, value[:, 1], value[:, 0])
        send[block] = jnp.where(odd, value[:, 0], value[:, 1]).astype(BF16)


def back_kernel(split, ids, *refs):
    parts, (before, gains), refs = refs[:8], refs[8:10], refs[10:]
    outs, others, buffer, sems, upstreams = refs[11:]
    downs = fetch(1, refs[:11], buffer, sems)
    ups = fetch(0, refs[:11], buffer, sems)
    for copy in downs.values():
        copy.start()
    rows, hidden = before.shape
    width = buffer.shape[1]
    for side in range(2):
        for at, flip in enumerate(FLIPS):
            upstreams[:, side * 4 + (ids[2] ^ flip)] = parts[side * 4 + at][...]
    total = jnp.zeros((rows, hidden), F32)
    for at in range(8):
        downs[at].wait()
        ups[at].start()
        block = ids[0] ^ at
        upstream = upstreams[block].reshape(rows, width)
        total = total + dot(upstream, buffer[8 + at], 1, 0)
    value = before[...]
    square = value * value
    bend = jnp.tanh(GELU_C * value * (1.0 + GELU_A * square))
    slope = 0.5 * (1.0 + bend) + 0.5 * GELU_C * value * (1.0 - bend * bend) * (
        1.0 + 3.0 * GELU_A * square
    )
    grad16 = (total * slope).astype(BF16)
    grad = grad16.astype(F32)
    first = jnp.sum(grad * gains[...], axis=1, keepdims=True)
    second = jnp.sum(grad * value, axis=1, keepdims=True)
    lane = lax.broadcasted_iota(jnp.int32, (rows, TAIL), 1)
    tail = jnp.where(lane == 0, first, jnp.where(lane == 1, second, 0.0))
    for copy in ups.values():
        copy.wait()
    if not split:
        others[...] = tail
        for at in range(8):
            outs[ids[0] ^ at] = dot(grad16, buffer[at], 1, 1)
        return
    for ref, core in ((others, 1 - ids[1]), (outs, ids[1])):
        for at in range(4):
            block = at // 2 * 4 + core * 2 + at % 2
            value = dot(grad16, buffer[ids[0] ^ block], 1, 1)
            ref[at // 2, at % 2, :, :width] = value.astype(ref.dtype)
            ref[at // 2, at % 2, :, width:] = tail.astype(ref.dtype)


def call(kernel, name, shapes, operands, weights=(), more=()):
    scratch = []
    if weights:
        scratch.append(pltpu.VMEM((16,) + weights[0].shape[1:], BF16))
        scratch.append(pltpu.SemaphoreType.DMA((16,)))
    scratch.extend(more)
    flops = 2 * 256 * 224 * 960 * 16 if weights else 0
    return pl.pallas_call(
        kernel,
        out_shape=shapes,
        in_specs=[SMEM] + [VMEM] * (len(operands) - 1) + [ANY] * len(weights),
        out_specs=tuple(VMEM for _ in shapes),
        scratch_shapes=scratch,
        compiler_params=PARAMS,
        cost_estimate=pl.CostEstimate(flops=flops, bytes_accessed=6 << 20, transcendentals=0),
        name=name,
    )(*operands, *weights)


def norm_stats(rows, axes):
    mean = jnp.mean(rows, axis=axes, keepdims=True)
    centered = rows - mean
    return mean, lax.rsqrt(jnp.mean(centered * centered, axis=axes, keepdims=True) + EPS)


def packed(data, sums):
    high = lax.reduce_precision(sums, 8, 7)
    tail = jnp.concatenate([high, sums - high], -1).astype(BF16)
    return jnp.concatenate([data.astype(BF16), jnp.broadcast_to(tail, data.shape[:-1] + (4,))], -1)


def unpacked(payload, cols):
    payload = payload.astype(F32)
    sums = payload[0, :, cols : cols + 2] + payload[0, :, cols + 2 : cols + 4]
    return payload[..., :cols], sums


def norm_back(grad, sums, rows, mean, inverse, gain, features):
    normed = (rows - mean) * inverse
    first, second = sums[:, 0:1] / features, sums[:, 1:2] / features
    return inverse * (grad * gain - first - normed * second)


def unit_rows(embed):
    inv = lax.rsqrt(jnp.sum(embed * embed, axis=1, keepdims=True) + EPS)
    return inv, (embed * inv).astype(BF16)


def unit_back(embed, inv, grad):
    along = jnp.sum(embed * grad, axis=1, keepdims=True)
    return inv * (grad - embed * (inv * inv) * along)


def gelu16(before):
    return jax.nn.gelu(before, approximate=True).astype(BF16)


def gelu_back16(before, grad):
    _, back = jax.vjp(lambda value: jax.nn.gelu(value, approximate=True), before)
    return back(grad)[0].astype(BF16)


def shards(
    image_in,
    text_in,
    image_gain,
    text_gain,
    image_up,
    image_down,
    text_up,
    text_down,
    image_head,
    log_scale,
    bias,
):
    img, grp = lax.axis_index("img"), lax.axis_index("grp")
    x, core = grp // 2, grp % 2
    members = lax.axis_size("img")
    top = members // 2
    rows, image_cols = image_in.shape
    quarter = rows // 4
    text_cols = text_in.shape[1]
    image_features, text_features = image_cols * 4, text_cols * 4
    width = image_features // members
    share_count = members // 4
    hidden_half = image_up.shape[1] // 2
    embed_width = image_head.shape[1]
    scale = jnp.exp(log_scale[0])
    shift = bias[0]
    ids = jnp.stack([img // top * 4 + img % 4, core, grp]).astype(jnp.int32)

    gate = lax.optimization_barrier

    with jax.named_scope("first"):
        shard = jnp.stack([image_up, image_down.T])
        low, high = shard[..., :hidden_half], shard[..., hidden_half:]
        both_halves = gate(jnp.stack([low, high]))
        far = widen(exchange(both_halves, img), img)
        near = widen(take(both_halves, img // top), img)
        near_y, near_z = swap(near, "img", 1), swap(near, "img", 2)
        text_x = swap(text_in, "grp", 2)
        text_parts = [text_in, text_x, swap(text_in, "grp", 1), swap(text_x, "grp", 1)]
        text_parts = place(text_parts, grp, FLIPS)
        text_whole = text_parts.transpose(1, 0, 2).reshape(rows, text_features).astype(F32)
        text_mean, text_inverse = norm_stats(text_whole, 1)
        text_normed = (text_whole - text_mean) * text_inverse
        text_before = dot((text_normed * text_gain).astype(BF16), text_up, 1, 0)
        text_branch = dot(gelu16(text_before), text_down, 1, 0)
        text_branch = text_branch.reshape(2, 2, quarter, text_features)
        send = take(text_branch, 1 - core, 1).astype(BF16)
        total = take(text_branch, core, 1) + swap(send, "grp", 1).astype(F32)
        send = take(total, 1 - x).astype(BF16)
        total = take(total, x) + swap(send, "grp", 2).astype(F32)
        own_in = image_in.reshape(rows, share_count, width).transpose(1, 0, 2)
        far_in = swap(own_in, "img", top)
        head_x = swap(image_head, "grp", 2)
        near_last = swap(near_z, "img", 1)
        far, near_y, near_z, near_last, total, far_in, head_x = gate(
            (far, near_y, near_z, near_last, total, far_in, head_x)
        )

    with jax.named_scope("second"):
        far_y = [swap(far[at], "img", 1) for at in (0, 1)]
        far_z = [swap(far[at], "img", 2) for at in (0, 1)]
        both = jnp.concatenate([own_in, far_in], 1)
        both = jnp.stack([both, swap(both, "grp", 2)])
        far_y, far_z, both = gate((far_y, far_z, both))

    with jax.named_scope("third"):
        far_last = [swap(far_z[0], "img", 1), swap(far_y[1], "img", 2)]
        weights = [near, near_y, near_z, far, near_last]
        for at in (0, 1):
            weights += [far_y[at], far_z[at], far_last[at]]
        both = jnp.concatenate([both, swap(both, "grp", 1)])
        text_embed = lax.dynamic_slice_in_dim(text_whole, grp * quarter, quarter, 0) + total
        text_inv, text_unit = unit_rows(text_embed)
        copies = jnp.broadcast_to(text_unit, (members,) + text_unit.shape)
        share = lax.all_to_all(copies, "img", split_axis=0, concat_axis=0, tiled=True)
        text_gains = jnp.sum(text_up.astype(F32) * text_gain[:, None], axis=0)
        share = share.reshape(members * quarter, embed_width)
        at = jnp.arange(members * quarter, dtype=jnp.int32)
        share_ids = at // quarter * rows + at % quarter
        text_ids = jnp.concatenate([share_ids + (grp ^ flip) * quarter for flip in FLIPS])

    with jax.named_scope("norm"):
        share_x = swap(share, "grp", 2)
        every = [share, share_x, swap(share, "grp", 1), swap(share_x, "grp", 1)]
        every_text = jnp.concatenate(every)
        heads = [image_head, head_x, swap(image_head, "grp", 1), swap(head_x, "grp", 1)]
        head = place(heads, grp, FLIPS).reshape(members, width, embed_width)
        gain = image_gain.reshape(members, 1, width)
        scaled, own_rows, mean, inverse = call(
            norm_kernel,
            "norm",
            (
                jax.ShapeDtypeStruct((members, 2 * rows + 16, width), BF16),
                jax.ShapeDtypeStruct((members, quarter, width), BF16),
                jax.ShapeDtypeStruct((2 * rows, 1), F32),
                jax.ShapeDtypeStruct((2 * rows, 1), F32),
            ),
            (ids, both, gain),
        )
        scaled = blocked(scaled)

    with jax.named_scope("image_forward"):
        shape = (8, 4, quarter, image_features // 8)
        (partial,) = call(
            up_kernel,
            "up",
            (jax.ShapeDtypeStruct((2 * rows + 16, hidden_half), F32),),
            (ids, scaled),
            weights[:7] + [weights[6]] * 4,
        )
        before, gains, keep, send = call(
            forward_kernel,
            "forward",
            (
                jax.ShapeDtypeStruct((2 * rows, hidden_half), F32),
                jax.ShapeDtypeStruct((1, hidden_half), F32),
                jax.ShapeDtypeStruct(shape, F32),
                jax.ShapeDtypeStruct(shape, BF16),
            ),
            (ids, scaled, tie(partial, share, head)),
            weights,
        )
        total = (keep + tie(swap(send, "grp", 1), share_x).astype(F32)).reshape(8, 2, 2, quarter, -1)
        send = take(total, 1 - x, 2).astype(BF16)
        got = swap(send, "grp", 2)
        total = take(total, x, 2) + got.astype(F32)
        branch = total[:, 0] + swap(total[:, 1].astype(BF16), "img", top).astype(F32)
        image_mid16 = (own_rows.astype(F32) + in_order(branch, members)).astype(BF16)
        image_mid16 = image_mid16.transpose(1, 0, 2).reshape(quarter, image_features)
        image_embed = dot(image_mid16, head.reshape(image_features, embed_width), 1, 0)
        image_inv, image_unit = unit_rows(image_embed)

    with jax.named_scope("image_loss"):
        image_ids = img * rows + grp * quarter + jnp.arange(quarter, dtype=jnp.int32)
        logits = scale * dot(image_unit, every_text, 1, 1) + shift
        same = (image_ids[:, None] == text_ids[None, :]).astype(F32)
        pull = (jax.nn.sigmoid(logits) - same).astype(BF16)
        grad_image_unit = scale * dot(pull, every_text, 1, 0)
        grad_embed16 = unit_back(image_embed, image_inv, grad_image_unit).astype(BF16)
        grad_mid16 = dot(grad_embed16, head.reshape(image_features, embed_width), 1, 1)
        grad_mid16 = grad_mid16.astype(BF16).reshape(quarter, members, width)
        grad_mid16 = blocked(grad_mid16.transpose(1, 0, 2))

    with jax.named_scope("text_loss"):
        unit_x = tie(swap(image_unit, "grp", 2), grad_embed16)
        pair = jnp.stack([image_unit, unit_x])
        image_units = jnp.concatenate([pair, swap(pair, "grp", 1)]).reshape(rows, embed_width)
        image_units = tie(image_units, grad_mid16)
        logits = scale * dot(image_units, share, 1, 1) + shift
        at = jnp.arange(quarter, dtype=jnp.int32)
        group_ids = jnp.concatenate([img * rows + (grp ^ flip) * quarter + at for flip in FLIPS])
        same = (group_ids[:, None] == (share_ids + grp * quarter)[None, :]).astype(F32)
        pull = (jax.nn.sigmoid(logits) - same).astype(BF16)
        text_partial = (scale * dot(pull, image_units, 0, 0)).astype(BF16)
        text_partial = text_partial.reshape(members, quarter, embed_width)
        text_parts = lax.all_to_all(
            text_partial, "img", split_axis=0, concat_axis=0, tiled=True
        )

    with jax.named_scope("image_backward"):
        far_grad = tie(swap(grad_mid16, "img", top), text_partial)
        sides = []
        for part in (grad_mid16, far_grad):
            part_x = swap(part, "grp", 2)
            sides += [part, part_x, swap(part, "grp", 1), swap(part_x, "grp", 1)]
        split = members == 8
        if split:
            shape = (2, share_count, 2 * rows, width + TAIL)
            shapes = (jax.ShapeDtypeStruct(shape, F32), jax.ShapeDtypeStruct(shape, BF16))
        else:
            shapes = (
                jax.ShapeDtypeStruct((8, 2 * rows, image_features // 8), F32),
                jax.ShapeDtypeStruct((2 * rows, TAIL), F32),
            )
        keep, send = call(
            functools.partial(back_kernel, split),
            "back",
            shapes,
            (ids, *sides, before, gains),
            weights,
            [pltpu.VMEM((8, 8, quarter, image_features // 8), BF16)],
        )
        if not split:
            tail = jnp.broadcast_to(send, (members,) + send.shape)
            total = jnp.concatenate([in_order(keep, members), tail], -1)
            total = total.reshape(2, 2, share_count, 2 * rows, width + TAIL)
            keep, send = take(total, core, 1), take(total, 1 - core, 1).astype(BF16)
        total = keep + tie(swap(send, "grp", 1), text_parts).astype(F32)
        send = take(total, 1 - x).astype(BF16)
        text_parts, send, own_parts = gate((text_parts, send, sides[:4]))
        total = take(total, x) + swap(send, "grp", 2).astype(F32)
        got = swap(total[:, rows:].astype(BF16), "img", top).astype(F32)
        total = total[:, :rows] + got
        total, sums = total[..., :width], total[0, :, width : width + 2]
        back = norm_back(
            total,
            sums,
            own_in.astype(F32),
            mean[:rows],
            inverse[:rows],
            take(gain.reshape(4, share_count, 1, width), grp),
            image_features,
        )
        own_grad = [
            take(in_order(part, members).reshape(4, share_count, quarter, width), grp)
            for part in own_parts
        ]
        own_grad = place(own_grad, grp, FLIPS).transpose(1, 0, 2, 3)
        own_grad = own_grad.reshape(share_count, rows, width)
        image_grad = (own_grad.astype(F32) + back).astype(BF16)
        image_grad = image_grad.transpose(1, 0, 2).reshape(rows, image_cols)

    with jax.named_scope("text_sum"):
        grad_text_unit = jnp.sum(text_parts.astype(F32), axis=0)
        grad_text16 = unit_back(text_embed, text_inv, grad_text_unit).astype(BF16)

    with jax.named_scope("text_backward"):
        pair = jnp.stack([grad_text16, swap(grad_text16, "grp", 2)])
        parts = jnp.concatenate([pair, swap(pair, "grp", 1)])
        upstream = place([parts[at] for at in range(4)], grp, FLIPS).reshape(rows, text_features)
        grad_before = gelu_back16(text_before, dot(upstream, text_down, 1, 1))
        grad32 = grad_before.astype(F32)
        sums = jnp.stack([jnp.sum(grad32 * text_gains, 1), jnp.sum(grad32 * text_before, 1)], 1)
        blocks = text_up.reshape(4, text_cols, -1)
        partial = {flip: dot(grad_before, take(blocks, grp ^ flip), 1, 1) for flip in FLIPS}
        send = jnp.stack([packed(partial[flip], sums) for flip in (1, 3)])
        data, more = unpacked(swap(send, "grp", 1), text_cols)
        sums = sums + more
        send = packed(partial[2] + data[1], sums)[None]
        more_data, more = unpacked(swap(send, "grp", 2), text_cols)
        total, sums = partial[0] + data[0] + more_data[0], sums + more
        own_gain = lax.dynamic_slice_in_dim(text_gain, grp * text_cols, text_cols, 0)
        back = norm_back(
            total, sums, text_in.astype(F32), text_mean, text_inverse, own_gain, text_features
        )
        own_grad = lax.dynamic_slice_in_dim(upstream, grp * text_cols, text_cols, 1)
        text_grad = (own_grad.astype(F32) + back).astype(BF16)
    return (image_grad, text_grad)


def solution(mesh):
    in_specs = (
        P("img", "grp"),
        P("img", "grp"),
        P(),
        P(),
        P("img", "grp"),
        P("grp", "img"),
        P(None, "grp"),
        P("grp", None),
        P("grp", None),
        P(),
        P(),
    )
    out_specs = (P("img", "grp"), P("img", "grp"))
    return jax.shard_map(shards, mesh=mesh, in_specs=in_specs, out_specs=out_specs, check_vma=False)
```

```python
import functools

import jax
import jax.numpy as jnp
from jax import lax
from jax.experimental import pallas as pl
from jax.experimental.pallas import tpu as pltpu
from jax.sharding import PartitionSpec as P

EPS = 1e-06
BF16 = jnp.bfloat16
F32 = jnp.float32
FLIPS = (0, 2, 1, 3)
GELU_C = 0.7978845608028654
GELU_A = 0.044715
VMEM = pl.BlockSpec(memory_space=pltpu.VMEM)
SMEM = pl.BlockSpec(memory_space=pltpu.SMEM)
ANY = pl.BlockSpec(memory_space=pl.ANY)
TAIL = 32
SLOTS = (0, 1, 2, 4, 3, 5, 6, 7)
PAIRED = 5
MEBIBYTES = {"norm": 12, "up": 18, "forward": 28, "back": 28}
PARAMS = pltpu.CompilerParams(vmem_limit_bytes=60 * 1024 * 1024)


def swap(value, axis, flip):
    return lax.ppermute(value, axis, [(i, i ^ flip) for i in range(lax.axis_size(axis))])


def place(parts, index, flips):
    whole = jnp.zeros((len(flips),) + parts[0].shape, parts[0].dtype)
    for part, flip in zip(parts, flips):
        whole = lax.dynamic_update_index_in_dim(whole, part, index ^ flip, 0)
    return whole


def tie(value, *events):
    return lax.optimization_barrier((value,) + events)[0]


def dot(left, right, left_dim, right_dim):
    dims = (((left_dim,), (right_dim,)), ((), ()))
    return lax.dot_general(left, right, dims, preferred_element_type=F32)


def take(array, index, axis=0):
    return lax.dynamic_index_in_dim(array, index, axis, False)


def exchange(halves, img):
    top = lax.axis_size("img") // 2
    pairs = [[at, at + top] for at in range(top)]
    got = lax.all_to_all(
        halves, "img", split_axis=0, concat_axis=0, tiled=True, axis_index_groups=pairs
    )
    return take(got, 1 - img // top)


def widen(block, img):
    members = lax.axis_size("img")
    held, flips, bit = block[None], [0], 4
    while bit < members // 2:
        held = jnp.concatenate([held, swap(held, "img", bit)])
        flips = flips + [flip ^ (bit // 4) for flip in flips]
        bit *= 2
    if len(flips) == 1:
        return block
    middle = img // 4 % (members // 8)
    held = place([held[at] for at in range(len(flips))], middle, flips)
    return held.transpose(1, 0, 2, 3).reshape(2, -1, block.shape[2])


def blocked(natural):
    members, rows, width = natural.shape
    if members == 8:
        return natural
    split = natural.reshape(2, members // 8, 4, rows, width)
    return split.transpose(0, 2, 3, 1, 4).reshape(8, rows, members // 8 * width)


def in_order(blocks, members):
    if members == 8:
        return blocks
    rows, width = blocks.shape[1], blocks.shape[2] * 8 // members
    split = blocks.reshape(2, 4, rows, members // 8, width)
    return split.transpose(0, 3, 1, 2, 4).reshape(members, rows, width)


def norm_kernel(ids, *refs):
    parts, (gain, scaled, own, mean, inverse) = refs[:4], refs[4:]
    share_count, rows, _ = parts[0].shape
    quarter = own.shape[1]
    features = float(4 * share_count * parts[0].shape[2])
    picks = [(at, sub) for at in range(4) for sub in range(share_count)]

    def sum_rows(term):
        return sum(
            jnp.sum(term(parts[at][sub].astype(F32)), axis=1, keepdims=True) for at, sub in picks
        )

    center = sum_rows(lambda value: value) / features
    variance = sum_rows(lambda value: (value - center) * (value - center)) / features
    factor = lax.rsqrt(variance + EPS)
    mean[...] = center
    inverse[...] = factor
    start = pl.multiple_of(ids[2] * quarter, quarter)
    for at, sub in picks:
        block = (ids[2] ^ FLIPS[at]) * share_count + sub
        value = parts[at][sub].astype(F32)
        scaled[block, :rows] = ((value - center) * factor * gain[block]).astype(BF16)
        own[block] = parts[at][sub, pl.ds(start, quarter)]
        rest = jnp.broadcast_to(gain[block], (16, gain.shape[2]))
        line = lax.broadcasted_iota(jnp.int32, rest.shape, 0)
        split = jnp.zeros_like(rest)
        for index in range(3):
            part = rest.astype(BF16).astype(F32)
            split = jnp.where(line == index, part, split)
            rest = rest - part
        scaled[block, rows:] = split.astype(BF16)


def fetch(which, blocks, buffer, sems):
    copies = []
    for at, block in zip(SLOTS, blocks[:5] + blocks[5 + 3 * which : 8 + 3 * which]):
        source, slot = block.at[which] if at in SLOTS[:PAIRED] else block, which * 8 + at
        copies.append((at, pltpu.make_async_copy(source, buffer.at[slot], sems.at[slot])))
    return dict(copies)


def up_kernel(ids, scaled, *refs):
    partial, buffer, sems = refs[11:]
    ups = fetch(0, refs[:11], buffer, sems)
    for at in range(7):
        ups[at].start()
    total = jnp.zeros(partial.shape, F32)
    for at in range(7):
        ups[at].wait()
        total = total + dot(scaled[ids[0] ^ at], buffer[at], 1, 0)
    partial[...] = total


def forward_kernel(ids, scaled, partial, *refs):
    before, gains, keep, send, buffer, sems = refs[11:]
    ups = fetch(0, refs[:11], buffer, sems)
    downs = fetch(1, refs[:11], buffer, sems)
    ups[7].start()
    for copy in downs.values():
        copy.start()
    rows = before.shape[0]
    ups[7].wait()
    total = partial[...] + dot(scaled[ids[0] ^ 7], buffer[7], 1, 0)
    value = total[:rows]
    before[...] = value
    bend = jnp.tanh(GELU_C * (value + GELU_A * value * value * value))
    hidden = (0.5 * value * (1.0 + bend)).astype(BF16)
    gains[...] = jnp.sum(total[rows:], axis=0, keepdims=True)
    _, pairs, quarter, width = keep.shape
    for at in range(8):
        downs[at].wait()
        block = ids[0] ^ at
        value = dot(hidden, buffer[8 + at], 1, 1).reshape(pairs, 2, quarter, width)
        odd = ids[1] == 1
        keep[block] = jnp.where(odd, value[:, 1], value[:, 0])
        send[block] = jnp.where(odd, value[:, 0], value[:, 1]).astype(BF16)


def back_kernel(split, ids, *refs):
    parts, (before, gains), refs = refs[:8], refs[8:10], refs[10:]
    outs, others, buffer, sems, upstreams = refs[11:]
    downs = fetch(1, refs[:11], buffer, sems)
    ups = fetch(0, refs[:11], buffer, sems)
    for copy in downs.values():
        copy.start()
    rows, hidden = before.shape
    width = buffer.shape[1]
    for side in range(2):
        for at, flip in enumerate(FLIPS):
            upstreams[:, side * 4 + (ids[2] ^ flip)] = parts[side * 4 + at][...]
    total = jnp.zeros((rows, hidden), F32)
    for at in range(8):
        downs[at].wait()
        ups[at].start()
        block = ids[0] ^ at
        upstream = upstreams[block].reshape(rows, width)
        total = total + dot(upstream, buffer[8 + at], 1, 0)
    value = before[...]
    square = value * value
    bend = jnp.tanh(GELU_C * value * (1.0 + GELU_A * square))
    slope = 0.5 * (1.0 + bend) + 0.5 * GELU_C * value * (1.0 - bend * bend) * (
        1.0 + 3.0 * GELU_A * square
    )
    grad16 = (total * slope).astype(BF16)
    grad = grad16.astype(F32)
    first = jnp.sum(grad * gains[...], axis=1, keepdims=True)
    second = jnp.sum(grad * value, axis=1, keepdims=True)
    lane = lax.broadcasted_iota(jnp.int32, (rows, TAIL), 1)
    tail = jnp.where(lane == 0, first, jnp.where(lane == 1, second, 0.0))
    for copy in ups.values():
        copy.wait()
    if not split:
        others[...] = tail
        for at in range(8):
            outs[ids[0] ^ at] = dot(grad16, buffer[at], 1, 1)
        return
    for ref, core in ((others, 1 - ids[1]), (outs, ids[1])):
        for at in range(4):
            block = at // 2 * 4 + core * 2 + at % 2
            value = dot(grad16, buffer[ids[0] ^ block], 1, 1)
            ref[at // 2, at % 2, :, :width] = value.astype(ref.dtype)
            ref[at // 2, at % 2, :, width:] = tail.astype(ref.dtype)


def call(kernel, name, shapes, operands, weights=(), more=()):
    scratch = []
    if weights:
        scratch.append(pltpu.VMEM((16,) + weights[0].shape[1:], BF16))
        scratch.append(pltpu.SemaphoreType.DMA((16,)))
    scratch.extend(more)
    flops = 2 * 256 * 224 * 960 * 16 if weights else 0
    return pl.pallas_call(
        kernel,
        out_shape=shapes,
        in_specs=[SMEM] + [VMEM] * (len(operands) - 1) + [ANY] * len(weights),
        out_specs=tuple(VMEM for _ in shapes),
        scratch_shapes=scratch,
        compiler_params=PARAMS,
        cost_estimate=pl.CostEstimate(
            flops=flops, bytes_accessed=MEBIBYTES[name] << 20, transcendentals=0
        ),
        name=name,
    )(*operands, *weights)


def norm_stats(rows, axes):
    mean = jnp.mean(rows, axis=axes, keepdims=True)
    centered = rows - mean
    return mean, lax.rsqrt(jnp.mean(centered * centered, axis=axes, keepdims=True) + EPS)


def packed(data, sums):
    high = lax.reduce_precision(sums, 8, 7)
    tail = jnp.concatenate([high, sums - high], -1).astype(BF16)
    return jnp.concatenate([data.astype(BF16), jnp.broadcast_to(tail, data.shape[:-1] + (4,))], -1)


def unpacked(payload, cols):
    payload = payload.astype(F32)
    sums = payload[0, :, cols : cols + 2] + payload[0, :, cols + 2 : cols + 4]
    return payload[..., :cols], sums


def norm_back(grad, sums, rows, mean, inverse, gain, features):
    normed = (rows - mean) * inverse
    first, second = sums[:, 0:1] / features, sums[:, 1:2] / features
    return inverse * (grad * gain - first - normed * second)


def unit_rows(embed):
    inv = lax.rsqrt(jnp.sum(embed * embed, axis=1, keepdims=True) + EPS)
    return inv, (embed * inv).astype(BF16)


def unit_back(embed, inv, grad):
    along = jnp.sum(embed * grad, axis=1, keepdims=True)
    return inv * (grad - embed * (inv * inv) * along)


def gelu16(before):
    return jax.nn.gelu(before, approximate=True).astype(BF16)


def gelu_back16(before, grad):
    _, back = jax.vjp(lambda value: jax.nn.gelu(value, approximate=True), before)
    return back(grad)[0].astype(BF16)


def shards(
    image_in,
    text_in,
    image_gain,
    text_gain,
    image_up,
    image_down,
    text_up,
    text_down,
    image_head,
    log_scale,
    bias,
):
    img, grp = lax.axis_index("img"), lax.axis_index("grp")
    x, core = grp // 2, grp % 2
    members = lax.axis_size("img")
    top = members // 2
    rows, image_cols = image_in.shape
    quarter = rows // 4
    text_cols = text_in.shape[1]
    image_features, text_features = image_cols * 4, text_cols * 4
    width = image_features // members
    share_count = members // 4
    hidden_half = image_up.shape[1] // 2
    embed_width = image_head.shape[1]
    scale = jnp.exp(log_scale[0])
    shift = bias[0]
    ids = jnp.stack([img // top * 4 + img % 4, core, grp]).astype(jnp.int32)

    gate = lax.optimization_barrier

    with jax.named_scope("first"):
        shard = jnp.stack([image_up, image_down.T])
        low, high = shard[..., :hidden_half], shard[..., hidden_half:]
        both_halves = gate(jnp.stack([low, high]))
        far = widen(exchange(both_halves, img), img)
        near = widen(take(both_halves, img // top), img)
        near_y, near_z = swap(near, "img", 1), swap(near, "img", 2)
        own_in = image_in.reshape(rows, share_count, width).transpose(1, 0, 2)
        far_in = swap(own_in, "img", top)
        text_x = swap(text_in, "grp", 2)
        text_parts = [text_in, text_x, swap(text_in, "grp", 1), swap(text_x, "grp", 1)]
        text_parts = place(text_parts, grp, FLIPS)
        text_whole = text_parts.transpose(1, 0, 2).reshape(rows, text_features).astype(F32)
        text_mean, text_inverse = norm_stats(text_whole, 1)
        text_normed = (text_whole - text_mean) * text_inverse
        text_before = dot((text_normed * text_gain).astype(BF16), text_up, 1, 0)
        text_branch = dot(gelu16(text_before), text_down, 1, 0)
        text_branch = text_branch.reshape(2, 2, quarter, text_features)
        send = take(text_branch, 1 - core, 1).astype(BF16)
        total = take(text_branch, core, 1) + swap(send, "grp", 1).astype(F32)
        send = take(total, 1 - x).astype(BF16)
        total = take(total, x) + swap(send, "grp", 2).astype(F32)
        head_x = swap(image_head, "grp", 2)
        near_last = swap(near_z, "img", 1)
        gain = image_gain.reshape(members, 1, width)
        text_gains = jnp.sum(text_up.astype(F32) * text_gain[:, None], axis=0)
        own_gain = lax.dynamic_slice_in_dim(text_gain, grp * text_cols, text_cols, 0)
        ready = (ids, gain, text_gains, own_gain)
        far, near_y, near_z, near_last, total, far_in, head_x, ready = gate(
            (far, near_y, near_z, near_last, total, far_in, head_x, ready)
        )
        ids, gain, text_gains, own_gain = ready

    with jax.named_scope("second"):
        far_parts, total = gate(([far[0], far[1]], total))
        far_y = [swap(part, "img", 1) for part in far_parts]
        far_z = [swap(part, "img", 2) for part in far_parts]
        both = jnp.concatenate([own_in, far_in], 1)
        both_x = swap(both, "grp", 2)
        total = tie(total, both_x)
        far_y, far_z, both, both_x = gate((far_y, far_z, both, both_x))
        parts = [both, both_x, swap(both, "grp", 1), swap(both_x, "grp", 1)]
        scaled, own_rows, mean, inverse = call(
            norm_kernel,
            "norm",
            (
                jax.ShapeDtypeStruct((members, 2 * rows + 16, width), BF16),
                jax.ShapeDtypeStruct((members, quarter, width), BF16),
                jax.ShapeDtypeStruct((2 * rows, 1), F32),
                jax.ShapeDtypeStruct((2 * rows, 1), F32),
            ),
            (ids, *parts, gain),
        )
        scaled = blocked(scaled)

    with jax.named_scope("third"):
        far_last = [swap(far_z[0], "img", 1), swap(far_y[1], "img", 2)]
        weights = [near, near_y, near_z, far, near_last]
        for at in (0, 1):
            weights += [far_y[at], far_z[at], far_last[at]]
        text_embed = lax.dynamic_slice_in_dim(text_whole, grp * quarter, quarter, 0) + total
        text_inv, text_unit = unit_rows(text_embed)
        copies = jnp.broadcast_to(text_unit, (top,) + text_unit.shape)
        lines = [list(range(first, members, 2)) for first in (0, 1)]
        line = lax.all_to_all(
            copies, "img", split_axis=0, concat_axis=0, tiled=True, axis_index_groups=lines
        )
        other = swap(line, "img", 1)
        odd = img % 2 == 1
        share = jnp.stack([jnp.where(odd, other, line), jnp.where(odd, line, other)], 1)
        share = share.reshape(members * quarter, embed_width)
        at = jnp.arange(members * quarter, dtype=jnp.int32)
        share_ids = at // quarter * rows + at % quarter
        text_ids = jnp.concatenate([share_ids + (grp ^ flip) * quarter for flip in FLIPS])

    with jax.named_scope("norm"):
        share_x = swap(share, "grp", 2)
        every = [share, share_x, swap(share, "grp", 1), swap(share_x, "grp", 1)]
        every_text = jnp.concatenate(every)
        heads = [image_head, head_x, swap(image_head, "grp", 1), swap(head_x, "grp", 1)]
        head = place(heads, grp, FLIPS).reshape(members, width, embed_width)

    with jax.named_scope("image_forward"):
        shape = (8, 4, quarter, image_features // 8)
        (partial,) = call(
            up_kernel,
            "up",
            (jax.ShapeDtypeStruct((2 * rows + 16, hidden_half), F32),),
            (ids, scaled),
            weights[:7] + [weights[6]] * 4,
        )
        before, gains, keep, send = call(
            forward_kernel,
            "forward",
            (
                jax.ShapeDtypeStruct((2 * rows, hidden_half), F32),
                jax.ShapeDtypeStruct((1, hidden_half), F32),
                jax.ShapeDtypeStruct(shape, F32),
                jax.ShapeDtypeStruct(shape, BF16),
            ),
            (ids, scaled, tie(partial, share, head)),
            weights,
        )
        total = (keep + swap(send, "grp", 1).astype(F32)).reshape(8, 2, 2, quarter, -1)
        send = tie(take(total, 1 - x, 2).astype(BF16), share_x)
        got = swap(send, "grp", 2)
        total = take(total, x, 2) + got.astype(F32)
        branch = total[:, 0] + swap(total[:, 1].astype(BF16), "img", top).astype(F32)
        image_mid16 = (own_rows.astype(F32) + in_order(branch, members)).astype(BF16)
        image_mid16 = image_mid16.transpose(1, 0, 2).reshape(quarter, image_features)
        image_embed = dot(image_mid16, head.reshape(image_features, embed_width), 1, 0)
        image_inv, image_unit = unit_rows(image_embed)

    with jax.named_scope("image_loss"):
        image_ids = img * rows + grp * quarter + jnp.arange(quarter, dtype=jnp.int32)
        logits = scale * dot(image_unit, every_text, 1, 1) + shift
        same = (image_ids[:, None] == text_ids[None, :]).astype(F32)
        pull = (jax.nn.sigmoid(logits) - same).astype(BF16)
        grad_image_unit = scale * dot(pull, every_text, 1, 0)
        grad_embed16 = unit_back(image_embed, image_inv, grad_image_unit).astype(BF16)
        grad_mid16 = dot(grad_embed16, head.reshape(image_features, embed_width), 1, 1)
        grad_mid16 = grad_mid16.astype(BF16).reshape(quarter, members, width)
        grad_mid16 = blocked(grad_mid16.transpose(1, 0, 2))

    with jax.named_scope("text_loss"):
        unit_x = tie(swap(image_unit, "grp", 2), grad_embed16)
        pair = jnp.stack([image_unit, unit_x])
        image_units = jnp.concatenate([pair, swap(pair, "grp", 1)]).reshape(rows, embed_width)
        image_units = tie(image_units, grad_mid16)
        logits = scale * dot(image_units, share, 1, 1) + shift
        at = jnp.arange(quarter, dtype=jnp.int32)
        group_ids = jnp.concatenate([img * rows + (grp ^ flip) * quarter + at for flip in FLIPS])
        same = (group_ids[:, None] == (share_ids + grp * quarter)[None, :]).astype(F32)
        pull = (jax.nn.sigmoid(logits) - same).astype(BF16)
        text_partial = (scale * dot(pull, image_units, 0, 0)).astype(BF16)
        text_partial = text_partial.reshape(members, quarter, embed_width)
        text_parts = lax.all_to_all(
            text_partial, "img", split_axis=0, concat_axis=0, tiled=True
        )

    with jax.named_scope("image_backward"):
        far_grad = tie(swap(grad_mid16, "img", top), text_partial)
        sides = []
        for part in (grad_mid16, far_grad):
            part_x = swap(part, "grp", 2)
            sides += [part, part_x, swap(part, "grp", 1), swap(part_x, "grp", 1)]
        split = members == 8
        if split:
            shape = (2, share_count, 2 * rows, width + TAIL)
            shapes = (jax.ShapeDtypeStruct(shape, F32), jax.ShapeDtypeStruct(shape, BF16))
        else:
            shapes = (
                jax.ShapeDtypeStruct((8, 2 * rows, image_features // 8), F32),
                jax.ShapeDtypeStruct((2 * rows, TAIL), F32),
            )
        keep, send = call(
            functools.partial(back_kernel, split),
            "back",
            shapes,
            (ids, *sides, before, gains),
            weights,
            [pltpu.VMEM((8, 8, quarter, image_features // 8), BF16)],
        )
        if not split:
            tail = jnp.broadcast_to(send, (members,) + send.shape)
            total = jnp.concatenate([in_order(keep, members), tail], -1)
            total = total.reshape(2, 2, share_count, 2 * rows, width + TAIL)
            keep, send = take(total, core, 1), take(total, 1 - core, 1).astype(BF16)
        total = keep + tie(swap(send, "grp", 1), text_parts).astype(F32)
        send = take(total, 1 - x).astype(BF16)
        text_parts, send, own_parts = gate((text_parts, send, sides[:4]))
        total = take(total, x) + swap(send, "grp", 2).astype(F32)
        got = swap(total[:, rows:].astype(BF16), "img", top).astype(F32)
        total = total[:, :rows] + got
        total, sums = total[..., :width], total[0, :, width : width + 2]
        back = norm_back(
            total,
            sums,
            own_in.astype(F32),
            mean[:rows],
            inverse[:rows],
            take(gain.reshape(4, share_count, 1, width), grp),
            image_features,
        )
        own_grad = [
            take(in_order(part, members).reshape(4, share_count, quarter, width), grp)
            for part in own_parts
        ]
        own_grad = place(own_grad, grp, FLIPS).transpose(1, 0, 2, 3)
        own_grad = own_grad.reshape(share_count, rows, width)
        image_grad = (own_grad.astype(F32) + back).astype(BF16)
        image_grad = image_grad.transpose(1, 0, 2).reshape(rows, image_cols)

    with jax.named_scope("text_sum"):
        grad_text_unit = jnp.sum(text_parts.astype(F32), axis=0)
        grad_text16 = unit_back(text_embed, text_inv, grad_text_unit).astype(BF16)

    with jax.named_scope("text_backward"):
        pair = jnp.stack([grad_text16, swap(grad_text16, "grp", 2)])
        parts = jnp.concatenate([pair, swap(pair, "grp", 1)])
        upstream = place([parts[at] for at in range(4)], grp, FLIPS).reshape(rows, text_features)
        grad_before = gelu_back16(text_before, dot(upstream, text_down, 1, 1))
        grad32 = grad_before.astype(F32)
        sums = jnp.stack([jnp.sum(grad32 * text_gains, 1), jnp.sum(grad32 * text_before, 1)], 1)
        blocks = text_up.reshape(4, text_cols, -1)
        partial = {flip: dot(grad_before, take(blocks, grp ^ flip), 1, 1) for flip in FLIPS}
        send = jnp.stack([packed(partial[flip], sums) for flip in (1, 3)])
        data, more = unpacked(swap(send, "grp", 1), text_cols)
        sums = sums + more
        send = packed(partial[2] + data[1], sums)[None]
        more_data, more = unpacked(swap(send, "grp", 2), text_cols)
        total, sums = partial[0] + data[0] + more_data[0], sums + more
        back = norm_back(
            total, sums, text_in.astype(F32), text_mean, text_inverse, own_gain, text_features
        )
        own_grad = lax.dynamic_slice_in_dim(upstream, grp * text_cols, text_cols, 1)
        text_grad = (own_grad.astype(F32) + back).astype(BF16)
    return (image_grad, text_grad)


def solution(mesh):
    in_specs = (
        P("img", "grp"),
        P("img", "grp"),
        P(),
        P(),
        P("img", "grp"),
        P("grp", "img"),
        P(None, "grp"),
        P("grp", None),
        P("grp", None),
        P(),
        P(),
    )
    out_specs = (P("img", "grp"), P("img", "grp"))
    return jax.shard_map(shards, mesh=mesh, in_specs=in_specs, out_specs=out_specs, check_vma=False)
```

```python
import functools

import jax
import jax.numpy as jnp
from jax import lax
from jax.experimental import pallas as pl
from jax.experimental.pallas import tpu as pltpu
from jax.sharding import PartitionSpec as P

EPS = 1e-06
BF16 = jnp.bfloat16
F32 = jnp.float32
FLIPS = (0, 2, 1, 3)
GELU_C = 0.7978845608028654
GELU_A = 0.044715
VMEM = pl.BlockSpec(memory_space=pltpu.VMEM)
SMEM = pl.BlockSpec(memory_space=pltpu.SMEM)
ANY = pl.BlockSpec(memory_space=pl.ANY)
TAIL = 32
SLOTS = (0, 1, 2, 4, 3, 5, 6, 7)
PAIRED = 5
MEBIBYTES = {"norm": 12, "up": 18, "forward": 28, "back": 28}
PARAMS = pltpu.CompilerParams(vmem_limit_bytes=63 * 1024 * 1024)


def swap(value, axis, flip):
    return lax.ppermute(value, axis, [(i, i ^ flip) for i in range(lax.axis_size(axis))])


def place(parts, index, flips):
    whole = jnp.zeros((len(flips),) + parts[0].shape, parts[0].dtype)
    for part, flip in zip(parts, flips):
        whole = lax.dynamic_update_index_in_dim(whole, part, index ^ flip, 0)
    return whole


def tie(value, *events):
    return lax.optimization_barrier((value,) + events)[0]


def dot(left, right, left_dim, right_dim):
    dims = (((left_dim,), (right_dim,)), ((), ()))
    return lax.dot_general(left, right, dims, preferred_element_type=F32)


def take(array, index, axis=0):
    return lax.dynamic_index_in_dim(array, index, axis, False)


def exchange(halves, img):
    top = lax.axis_size("img") // 2
    pairs = [[at, at + top] for at in range(top)]
    got = lax.all_to_all(
        halves, "img", split_axis=0, concat_axis=0, tiled=True, axis_index_groups=pairs
    )
    return take(got, 1 - img // top)


def widen(block, img):
    members = lax.axis_size("img")
    held, flips, bit = block[None], [0], 4
    while bit < members // 2:
        held = jnp.concatenate([held, swap(held, "img", bit)])
        flips = flips + [flip ^ (bit // 4) for flip in flips]
        bit *= 2
    if len(flips) == 1:
        return block
    middle = img // 4 % (members // 8)
    held = place([held[at] for at in range(len(flips))], middle, flips)
    return held.transpose(1, 0, 2, 3).reshape(2, -1, block.shape[2])


def blocked(natural):
    members, rows, width = natural.shape
    if members == 8:
        return natural
    split = natural.reshape(2, members // 8, 4, rows, width)
    return split.transpose(0, 2, 3, 1, 4).reshape(8, rows, members // 8 * width)


def in_order(blocks, members):
    if members == 8:
        return blocks
    rows, width = blocks.shape[1], blocks.shape[2] * 8 // members
    split = blocks.reshape(2, 4, rows, members // 8, width)
    return split.transpose(0, 3, 1, 2, 4).reshape(members, rows, width)


def norm_kernel(ids, *refs):
    parts, (gain, scaled, own, mean, inverse) = refs[:4], refs[4:]
    share_count, rows, _ = parts[0].shape
    quarter = own.shape[1]
    features = float(4 * share_count * parts[0].shape[2])
    picks = [(at, sub) for at in range(4) for sub in range(share_count)]

    def sum_rows(term):
        return sum(
            jnp.sum(term(parts[at][sub].astype(F32)), axis=1, keepdims=True) for at, sub in picks
        )

    center = sum_rows(lambda value: value) / features
    variance = sum_rows(lambda value: (value - center) * (value - center)) / features
    factor = lax.rsqrt(variance + EPS)
    mean[...] = center
    inverse[...] = factor
    start = pl.multiple_of(ids[2] * quarter, quarter)
    for at, sub in picks:
        block = (ids[2] ^ FLIPS[at]) * share_count + sub
        value = parts[at][sub].astype(F32)
        scaled[block, :rows] = ((value - center) * factor * gain[block]).astype(BF16)
        own[block] = parts[at][sub, pl.ds(start, quarter)]
        rest = jnp.broadcast_to(gain[block], (16, gain.shape[2]))
        line = lax.broadcasted_iota(jnp.int32, rest.shape, 0)
        split = jnp.zeros_like(rest)
        for index in range(3):
            part = rest.astype(BF16).astype(F32)
            split = jnp.where(line == index, part, split)
            rest = rest - part
        scaled[block, rows:] = split.astype(BF16)


def fetch(which, blocks, buffer, sems):
    copies = []
    for at, block in zip(SLOTS, blocks[:5] + blocks[5 + 3 * which : 8 + 3 * which]):
        source, slot = block.at[which] if at in SLOTS[:PAIRED] else block, which * 8 + at
        copies.append((at, pltpu.make_async_copy(source, buffer.at[slot], sems.at[slot])))
    return dict(copies)


def up_kernel(ids, scaled, *refs):
    partial, buffer, sems = refs[11:]
    ups = fetch(0, refs[:11], buffer, sems)
    for at in range(7):
        ups[at].start()
    total = jnp.zeros(partial.shape, F32)
    for at in range(7):
        ups[at].wait()
        total = total + dot(scaled[ids[0] ^ at], buffer[at], 1, 0)
    partial[...] = total


def forward_kernel(ids, scaled, partial, *refs):
    before, gains, keep, send, buffer, sems = refs[11:]
    ups = fetch(0, refs[:11], buffer, sems)
    downs = fetch(1, refs[:11], buffer, sems)
    ups[7].start()
    for copy in downs.values():
        copy.start()
    rows = before.shape[0]
    ups[7].wait()
    total = partial[...] + dot(scaled[ids[0] ^ 7], buffer[7], 1, 0)
    value = total[:rows]
    before[...] = value
    bend = jnp.tanh(GELU_C * (value + GELU_A * value * value * value))
    hidden = (0.5 * value * (1.0 + bend)).astype(BF16)
    gains[...] = jnp.sum(total[rows:], axis=0, keepdims=True)
    _, pairs, quarter, width = keep.shape
    for at in range(8):
        downs[at].wait()
        block = ids[0] ^ at
        value = dot(hidden, buffer[8 + at], 1, 1).reshape(pairs, 2, quarter, width)
        odd = ids[1] == 1
        keep[block] = jnp.where(odd, value[:, 1], value[:, 0])
        send[block] = jnp.where(odd, value[:, 0], value[:, 1]).astype(BF16)


def back_kernel(split, ids, *refs):
    parts, (before, gains), refs = refs[:8], refs[8:10], refs[10:]
    outs, others, buffer, sems, upstreams = refs[11:]
    downs = fetch(1, refs[:11], buffer, sems)
    ups = fetch(0, refs[:11], buffer, sems)
    for copy in downs.values():
        copy.start()
    rows, hidden = before.shape
    width = buffer.shape[1]
    for side in range(2):
        for at, flip in enumerate(FLIPS):
            upstreams[:, side * 4 + (ids[2] ^ flip)] = parts[side * 4 + at][...]
    total = jnp.zeros((rows, hidden), F32)
    for at in range(8):
        downs[at].wait()
        ups[at].start()
        block = ids[0] ^ at
        upstream = upstreams[block].reshape(rows, width)
        total = total + dot(upstream, buffer[8 + at], 1, 0)
    value = before[...]
    square = value * value
    bend = jnp.tanh(GELU_C * value * (1.0 + GELU_A * square))
    slope = 0.5 * (1.0 + bend) + 0.5 * GELU_C * value * (1.0 - bend * bend) * (
        1.0 + 3.0 * GELU_A * square
    )
    grad16 = (total * slope).astype(BF16)
    grad = grad16.astype(F32)
    first = jnp.sum(grad * gains[...], axis=1, keepdims=True)
    second = jnp.sum(grad * value, axis=1, keepdims=True)
    lane = lax.broadcasted_iota(jnp.int32, (rows, TAIL), 1)
    tail = jnp.where(lane == 0, first, jnp.where(lane == 1, second, 0.0))
    for copy in ups.values():
        copy.wait()
    if not split:
        others[...] = tail
        for at in range(8):
            outs[ids[0] ^ at] = dot(grad16, buffer[at], 1, 1)
        return
    for ref, core in ((others, 1 - ids[1]), (outs, ids[1])):
        for at in range(4):
            block = at // 2 * 4 + core * 2 + at % 2
            value = dot(grad16, buffer[ids[0] ^ block], 1, 1)
            ref[at // 2, at % 2, :, :width] = value.astype(ref.dtype)
            ref[at // 2, at % 2, :, width:] = tail.astype(ref.dtype)


def call(kernel, name, shapes, operands, weights=(), more=()):
    scratch = []
    if weights:
        scratch.append(pltpu.VMEM((16,) + weights[0].shape[1:], BF16))
        scratch.append(pltpu.SemaphoreType.DMA((16,)))
    scratch.extend(more)
    flops = 2 * 256 * 224 * 960 * 16 if weights else 0
    return pl.pallas_call(
        kernel,
        out_shape=shapes,
        in_specs=[SMEM] + [VMEM] * (len(operands) - 1) + [ANY] * len(weights),
        out_specs=tuple(VMEM for _ in shapes),
        scratch_shapes=scratch,
        compiler_params=PARAMS,
        cost_estimate=pl.CostEstimate(
            flops=flops, bytes_accessed=MEBIBYTES[name] << 20, transcendentals=0
        ),
        name=name,
    )(*operands, *weights)


def norm_stats(rows, axes):
    mean = jnp.mean(rows, axis=axes, keepdims=True)
    centered = rows - mean
    return mean, lax.rsqrt(jnp.mean(centered * centered, axis=axes, keepdims=True) + EPS)


def packed(data, sums):
    high = lax.reduce_precision(sums, 8, 7)
    tail = jnp.concatenate([high, sums - high], -1).astype(BF16)
    return jnp.concatenate([data.astype(BF16), jnp.broadcast_to(tail, data.shape[:-1] + (4,))], -1)


def unpacked(payload, cols):
    payload = payload.astype(F32)
    sums = payload[0, :, cols : cols + 2] + payload[0, :, cols + 2 : cols + 4]
    return payload[..., :cols], sums


def norm_back(grad, sums, rows, mean, inverse, gain, features):
    normed = (rows - mean) * inverse
    first, second = sums[:, 0:1] / features, sums[:, 1:2] / features
    return inverse * (grad * gain - first - normed * second)


def unit_rows(embed):
    inv = lax.rsqrt(jnp.sum(embed * embed, axis=1, keepdims=True) + EPS)
    return inv, (embed * inv).astype(BF16)


def unit_back(embed, inv, grad):
    along = jnp.sum(embed * grad, axis=1, keepdims=True)
    return inv * (grad - embed * (inv * inv) * along)


def gelu16(before):
    return jax.nn.gelu(before, approximate=True).astype(BF16)


def gelu_back16(before, grad):
    _, back = jax.vjp(lambda value: jax.nn.gelu(value, approximate=True), before)
    return back(grad)[0].astype(BF16)


def shards(
    image_in,
    text_in,
    image_gain,
    text_gain,
    image_up,
    image_down,
    text_up,
    text_down,
    image_head,
    log_scale,
    bias,
):
    img, grp = lax.axis_index("img"), lax.axis_index("grp")
    x, core = grp // 2, grp % 2
    members = lax.axis_size("img")
    top = members // 2
    rows, image_cols = image_in.shape
    quarter = rows // 4
    text_cols = text_in.shape[1]
    image_features, text_features = image_cols * 4, text_cols * 4
    width = image_features // members
    share_count = members // 4
    hidden_half = image_up.shape[1] // 2
    embed_width = image_head.shape[1]
    scale = jnp.exp(log_scale[0])
    shift = bias[0]
    ids = jnp.stack([img // top * 4 + img % 4, core, grp]).astype(jnp.int32)

    gate = lax.optimization_barrier

    with jax.named_scope("first"):
        shard = jnp.stack([image_up, image_down.T])
        low, high = shard[..., :hidden_half], shard[..., hidden_half:]
        both_halves = gate(jnp.stack([low, high]))
        far = widen(exchange(both_halves, img), img)
        near = widen(take(both_halves, img // top), img)
        near_y, near_z = swap(near, "img", 1), swap(near, "img", 2)
        own_in = image_in.reshape(rows, share_count, width).transpose(1, 0, 2)
        far_in = swap(own_in, "img", top)
        text_x = swap(text_in, "grp", 2)
        text_parts = [text_in, text_x, swap(text_in, "grp", 1), swap(text_x, "grp", 1)]
        text_parts = place(text_parts, grp, FLIPS)
        text_whole = text_parts.transpose(1, 0, 2).reshape(rows, text_features).astype(F32)
        text_mean, text_inverse = norm_stats(text_whole, 1)
        text_normed = (text_whole - text_mean) * text_inverse
        text_before = dot((text_normed * text_gain).astype(BF16), text_up, 1, 0)
        text_branch = dot(gelu16(text_before), text_down, 1, 0)
        text_branch = text_branch.reshape(2, 2, quarter, text_features)
        send = take(text_branch, 1 - core, 1).astype(BF16)
        total = take(text_branch, core, 1) + swap(send, "grp", 1).astype(F32)
        send = take(total, 1 - x).astype(BF16)
        total = take(total, x) + swap(send, "grp", 2).astype(F32)
        head_x = swap(image_head, "grp", 2)
        near_last = swap(near_z, "img", 1)
        gain = image_gain.reshape(members, 1, width)
        text_gains = jnp.sum(text_up.astype(F32) * text_gain[:, None], axis=0)
        own_gain = lax.dynamic_slice_in_dim(text_gain, grp * text_cols, text_cols, 0)
        ready = (ids, gain, text_gains, own_gain, scale, shift)
        far, near_y, near_z, near_last, total, far_in, head_x, ready = gate(
            (far, near_y, near_z, near_last, total, far_in, head_x, ready)
        )
        ids, gain, text_gains, own_gain, scale, shift = ready

    with jax.named_scope("second"):
        far_parts, total = gate(([far[0], far[1]], total))
        far_y = [swap(part, "img", 1) for part in far_parts]
        far_z = [swap(part, "img", 2) for part in far_parts]
        both = jnp.concatenate([own_in, far_in], 1)
        both_x = swap(both, "grp", 2)
        total = tie(total, both_x)
        far_y, far_z, both, both_x = gate((far_y, far_z, both, both_x))
        parts = [both, both_x, swap(both, "grp", 1), swap(both_x, "grp", 1)]
        scaled, own_rows, mean, inverse = call(
            norm_kernel,
            "norm",
            (
                jax.ShapeDtypeStruct((members, 2 * rows + 16, width), BF16),
                jax.ShapeDtypeStruct((members, quarter, width), BF16),
                jax.ShapeDtypeStruct((2 * rows, 1), F32),
                jax.ShapeDtypeStruct((2 * rows, 1), F32),
            ),
            (ids, *parts, gain),
        )
        scaled = blocked(scaled)

    with jax.named_scope("third"):
        far_last = [swap(far_z[0], "img", 1), swap(far_y[1], "img", 2)]
        weights = [near, near_y, near_z, far, near_last]
        for at in (0, 1):
            weights += [far_y[at], far_z[at], far_last[at]]
        text_embed = lax.dynamic_slice_in_dim(text_whole, grp * quarter, quarter, 0) + total
        text_inv, text_unit = unit_rows(text_embed)
        copies = jnp.broadcast_to(text_unit, (top,) + text_unit.shape)
        lines = [list(range(first, members, 2)) for first in (0, 1)]
        line = lax.all_to_all(
            copies, "img", split_axis=0, concat_axis=0, tiled=True, axis_index_groups=lines
        )
        other = swap(line, "img", 1)
        odd = img % 2 == 1
        share = jnp.stack([jnp.where(odd, other, line), jnp.where(odd, line, other)], 1)
        share = share.reshape(members * quarter, embed_width)
        at = jnp.arange(members * quarter, dtype=jnp.int32)
        share_ids = at // quarter * rows + at % quarter
        text_ids = jnp.concatenate([share_ids + (grp ^ flip) * quarter for flip in FLIPS])

    with jax.named_scope("norm"):
        share_x = swap(share, "grp", 2)
        every = [share, share_x, swap(share, "grp", 1), swap(share_x, "grp", 1)]
        every_text = jnp.concatenate(every)
        heads = [image_head, head_x, swap(image_head, "grp", 1), swap(head_x, "grp", 1)]
        head = place(heads, grp, FLIPS).reshape(members, width, embed_width)

    with jax.named_scope("image_forward"):
        shape = (8, 4, quarter, image_features // 8)
        (partial,) = call(
            up_kernel,
            "up",
            (jax.ShapeDtypeStruct((2 * rows + 16, hidden_half), F32),),
            (ids, scaled),
            weights[:7] + [weights[6]] * 4,
        )
        before, gains, keep, send = call(
            forward_kernel,
            "forward",
            (
                jax.ShapeDtypeStruct((2 * rows, hidden_half), F32),
                jax.ShapeDtypeStruct((1, hidden_half), F32),
                jax.ShapeDtypeStruct(shape, F32),
                jax.ShapeDtypeStruct(shape, BF16),
            ),
            (ids, scaled, tie(partial, share, head)),
            weights,
        )
        total = (keep + swap(send, "grp", 1).astype(F32)).reshape(8, 2, 2, quarter, -1)
        send = tie(take(total, 1 - x, 2).astype(BF16), share_x)
        got = swap(send, "grp", 2)
        total = take(total, x, 2) + got.astype(F32)
        branch = total[:, 0] + swap(total[:, 1].astype(BF16), "img", top).astype(F32)
        image_mid16 = (own_rows.astype(F32) + in_order(branch, members)).astype(BF16)
        image_mid16 = image_mid16.transpose(1, 0, 2).reshape(quarter, image_features)
        image_embed = dot(image_mid16, head.reshape(image_features, embed_width), 1, 0)
        image_inv, image_unit = unit_rows(image_embed)

    with jax.named_scope("image_loss"):
        image_ids = img * rows + grp * quarter + jnp.arange(quarter, dtype=jnp.int32)
        logits = scale * dot(image_unit, every_text, 1, 1) + shift
        same = (image_ids[:, None] == text_ids[None, :]).astype(F32)
        pull = (jax.nn.sigmoid(logits) - same).astype(BF16)
        grad_image_unit = scale * dot(pull, every_text, 1, 0)
        grad_embed16 = unit_back(image_embed, image_inv, grad_image_unit).astype(BF16)
        grad_mid16 = dot(grad_embed16, head.reshape(image_features, embed_width), 1, 1)
        grad_mid16 = grad_mid16.astype(BF16).reshape(quarter, members, width)
        grad_mid16 = blocked(grad_mid16.transpose(1, 0, 2))

    with jax.named_scope("text_loss"):
        unit_x = tie(swap(image_unit, "grp", 2), grad_embed16)
        pair = jnp.stack([image_unit, unit_x])
        image_units = jnp.concatenate([pair, swap(pair, "grp", 1)]).reshape(rows, embed_width)
        image_units = tie(image_units, grad_mid16)
        logits = scale * dot(image_units, share, 1, 1) + shift
        at = jnp.arange(quarter, dtype=jnp.int32)
        group_ids = jnp.concatenate([img * rows + (grp ^ flip) * quarter + at for flip in FLIPS])
        same = (group_ids[:, None] == (share_ids + grp * quarter)[None, :]).astype(F32)
        pull = (jax.nn.sigmoid(logits) - same).astype(BF16)
        text_partial = (scale * dot(pull, image_units, 0, 0)).astype(BF16)
        text_partial = text_partial.reshape(members, quarter, embed_width)
        text_parts = lax.all_to_all(
            text_partial, "img", split_axis=0, concat_axis=0, tiled=True
        )

    with jax.named_scope("image_backward"):
        far_grad = tie(swap(grad_mid16, "img", top), text_partial)
        sides = []
        for part in (grad_mid16, far_grad):
            part_x = swap(part, "grp", 2)
            sides += [part, part_x, swap(part, "grp", 1), swap(part_x, "grp", 1)]
        split = members == 8
        if split:
            shape = (2, share_count, 2 * rows, width + TAIL)
            shapes = (jax.ShapeDtypeStruct(shape, F32), jax.ShapeDtypeStruct(shape, BF16))
        else:
            shapes = (
                jax.ShapeDtypeStruct((8, 2 * rows, image_features // 8), F32),
                jax.ShapeDtypeStruct((2 * rows, TAIL), F32),
            )
        keep, send = call(
            functools.partial(back_kernel, split),
            "back",
            shapes,
            (ids, *sides, before, gains),
            weights,
            [pltpu.VMEM((8, 8, quarter, image_features // 8), BF16)],
        )
        if not split:
            tail = jnp.broadcast_to(send, (members,) + send.shape)
            total = jnp.concatenate([in_order(keep, members), tail], -1)
            total = total.reshape(2, 2, share_count, 2 * rows, width + TAIL)
            keep, send = take(total, core, 1), take(total, 1 - core, 1).astype(BF16)
        total = keep + tie(swap(send, "grp", 1), text_parts).astype(F32)
        send = take(total, 1 - x).astype(BF16)
        text_parts, send, own_parts = gate((text_parts, send, sides[:4]))
        total = take(total, x) + swap(send, "grp", 2).astype(F32)
        got = swap(total[:, rows:].astype(BF16), "img", top).astype(F32)
        total = total[:, :rows] + got
        total, sums = total[..., :width], total[0, :, width : width + 2]
        back = norm_back(
            total,
            sums,
            own_in.astype(F32),
            mean[:rows],
            inverse[:rows],
            take(gain.reshape(4, share_count, 1, width), grp),
            image_features,
        )
        own_grad = [
            take(in_order(part, members).reshape(4, share_count, quarter, width), grp)
            for part in own_parts
        ]
        own_grad = place(own_grad, grp, FLIPS).transpose(1, 0, 2, 3)
        own_grad = own_grad.reshape(share_count, rows, width)
        image_grad = (own_grad.astype(F32) + back).astype(BF16)
        image_grad = jnp.concatenate([image_grad[at] for at in range(share_count)], 1)

    with jax.named_scope("text_sum"):
        grad_text_unit = jnp.sum(text_parts.astype(F32), axis=0)
        grad_text16 = unit_back(text_embed, text_inv, grad_text_unit).astype(BF16)

    with jax.named_scope("text_backward"):
        pair = jnp.stack([grad_text16, swap(grad_text16, "grp", 2)])
        parts = jnp.concatenate([pair, swap(pair, "grp", 1)])
        upstream = place([parts[at] for at in range(4)], grp, FLIPS).reshape(rows, text_features)
        grad_before = gelu_back16(text_before, dot(upstream, text_down, 1, 1))
        grad32 = grad_before.astype(F32)
        sums = jnp.stack([jnp.sum(grad32 * text_gains, 1), jnp.sum(grad32 * text_before, 1)], 1)
        blocks = text_up.reshape(4, text_cols, -1)
        partial = {flip: dot(grad_before, take(blocks, grp ^ flip), 1, 1) for flip in FLIPS}
        send = jnp.stack([packed(partial[flip], sums) for flip in (1, 3)])
        data, more = unpacked(swap(send, "grp", 1), text_cols)
        sums = sums + more
        send = packed(partial[2] + data[1], sums)[None]
        more_data, more = unpacked(swap(send, "grp", 2), text_cols)
        total, sums = partial[0] + data[0] + more_data[0], sums + more
        back = norm_back(
            total, sums, text_in.astype(F32), text_mean, text_inverse, own_gain, text_features
        )
        own_grad = lax.dynamic_slice_in_dim(upstream, grp * text_cols, text_cols, 1)
        text_grad = (own_grad.astype(F32) + back).astype(BF16)
    return (image_grad, text_grad)


def solution(mesh):
    in_specs = (
        P("img", "grp"),
        P("img", "grp"),
        P(),
        P(),
        P("img", "grp"),
        P("grp", "img"),
        P(None, "grp"),
        P("grp", None),
        P("grp", None),
        P(),
        P(),
    )
    out_specs = (P("img", "grp"), P("img", "grp"))
    return jax.shard_map(shards, mesh=mesh, in_specs=in_specs, out_specs=out_specs, check_vma=False)
```

```python
import functools

import jax
import jax.numpy as jnp
from jax import lax
from jax.experimental import pallas as pl
from jax.experimental.pallas import tpu as pltpu
from jax.sharding import PartitionSpec as P

EPS = 1e-06
BF16 = jnp.bfloat16
F32 = jnp.float32
FLIPS = (0, 2, 1, 3)
GELU_C = 0.7978845608028654
GELU_A = 0.044715
VMEM = pl.BlockSpec(memory_space=pltpu.VMEM)
SMEM = pl.BlockSpec(memory_space=pltpu.SMEM)
ANY = pl.BlockSpec(memory_space=pl.ANY)
TAIL = 32
SLOTS = (0, 1, 2, 4, 3, 5, 6, 7)
PAIRED = 5
MEBIBYTES = {"norm": 12, "up": 18, "forward": 28, "back": 28}
PARAMS = pltpu.CompilerParams(vmem_limit_bytes=63 * 1024 * 1024)


def swap(value, axis, flip):
    return lax.ppermute(value, axis, [(i, i ^ flip) for i in range(lax.axis_size(axis))])


def place(parts, index, flips):
    whole = jnp.zeros((len(flips),) + parts[0].shape, parts[0].dtype)
    for part, flip in zip(parts, flips):
        whole = lax.dynamic_update_index_in_dim(whole, part, index ^ flip, 0)
    return whole


def tie(value, *events):
    return lax.optimization_barrier((value,) + events)[0]


def dot(left, right, left_dim, right_dim):
    dims = (((left_dim,), (right_dim,)), ((), ()))
    return lax.dot_general(left, right, dims, preferred_element_type=F32)


def take(array, index, axis=0):
    return lax.dynamic_index_in_dim(array, index, axis, False)


def exchange(halves, img):
    top = lax.axis_size("img") // 2
    pairs = [[at, at + top] for at in range(top)]
    got = lax.all_to_all(
        halves, "img", split_axis=0, concat_axis=0, tiled=True, axis_index_groups=pairs
    )
    return take(got, 1 - img // top)


def widen(block, img):
    members = lax.axis_size("img")
    held, flips, bit = block[None], [0], 4
    while bit < members // 2:
        held = jnp.concatenate([held, swap(held, "img", bit)])
        flips = flips + [flip ^ (bit // 4) for flip in flips]
        bit *= 2
    if len(flips) == 1:
        return block
    middle = img // 4 % (members // 8)
    held = place([held[at] for at in range(len(flips))], middle, flips)
    return held.transpose(1, 0, 2, 3).reshape(2, -1, block.shape[2])


def blocked(natural):
    members, rows, width = natural.shape
    if members == 8:
        return natural
    split = natural.reshape(2, members // 8, 4, rows, width)
    return split.transpose(0, 2, 3, 1, 4).reshape(8, rows, members // 8 * width)


def in_order(blocks, members):
    if members == 8:
        return blocks
    rows, width = blocks.shape[1], blocks.shape[2] * 8 // members
    split = blocks.reshape(2, 4, rows, members // 8, width)
    return split.transpose(0, 3, 1, 2, 4).reshape(members, rows, width)


def norm_kernel(ids, *refs):
    parts, (gain, scaled, own, mean, inverse) = refs[:4], refs[4:]
    share_count, rows, _ = parts[0].shape
    quarter = own.shape[1]
    features = float(4 * share_count * parts[0].shape[2])
    picks = [(at, sub) for at in range(4) for sub in range(share_count)]

    def sum_rows(term):
        return sum(
            jnp.sum(term(parts[at][sub].astype(F32)), axis=1, keepdims=True) for at, sub in picks
        )

    center = sum_rows(lambda value: value) / features
    variance = sum_rows(lambda value: (value - center) * (value - center)) / features
    factor = lax.rsqrt(variance + EPS)
    mean[...] = center
    inverse[...] = factor
    start = pl.multiple_of(ids[2] * quarter, quarter)
    for at, sub in picks:
        block = (ids[2] ^ FLIPS[at]) * share_count + sub
        value = parts[at][sub].astype(F32)
        scaled[block, :rows] = ((value - center) * factor * gain[block]).astype(BF16)
        own[block] = parts[at][sub, pl.ds(start, quarter)]
        rest = jnp.broadcast_to(gain[block], (16, gain.shape[2]))
        line = lax.broadcasted_iota(jnp.int32, rest.shape, 0)
        split = jnp.zeros_like(rest)
        for index in range(3):
            part = rest.astype(BF16).astype(F32)
            split = jnp.where(line == index, part, split)
            rest = rest - part
        scaled[block, rows:] = split.astype(BF16)


def fetch(which, blocks, buffer, sems):
    copies = []
    for at, block in zip(SLOTS, blocks[:5] + blocks[5 + 3 * which : 8 + 3 * which]):
        source, slot = block.at[which] if at in SLOTS[:PAIRED] else block, which * 8 + at
        copies.append((at, pltpu.make_async_copy(source, buffer.at[slot], sems.at[slot])))
    return dict(copies)


def up_kernel(ids, scaled, *refs):
    partial, buffer, sems = refs[11:]
    ups = fetch(0, refs[:11], buffer, sems)
    for at in range(7):
        ups[at].start()
    total = jnp.zeros(partial.shape, F32)
    for at in range(7):
        ups[at].wait()
        total = total + dot(scaled[ids[0] ^ at], buffer[at], 1, 0)
    partial[...] = total


def forward_kernel(ids, scaled, partial, *refs):
    before, gains, keep, send, buffer, sems = refs[11:]
    ups = fetch(0, refs[:11], buffer, sems)
    downs = fetch(1, refs[:11], buffer, sems)
    ups[7].start()
    for copy in downs.values():
        copy.start()
    rows = before.shape[0]
    ups[7].wait()
    total = partial[...] + dot(scaled[ids[0] ^ 7], buffer[7], 1, 0)
    value = total[:rows]
    before[...] = value
    bend = jnp.tanh(GELU_C * (value + GELU_A * value * value * value))
    hidden = (0.5 * value * (1.0 + bend)).astype(BF16)
    gains[...] = jnp.sum(total[rows:], axis=0, keepdims=True)
    _, pairs, quarter, width = keep.shape
    for at in range(8):
        downs[at].wait()
        block = ids[0] ^ at
        value = dot(hidden, buffer[8 + at], 1, 1).reshape(pairs, 2, quarter, width)
        odd = ids[1] == 1
        keep[block] = jnp.where(odd, value[:, 1], value[:, 0])
        send[block] = jnp.where(odd, value[:, 0], value[:, 1]).astype(BF16)


def back_kernel(split, ids, *refs):
    parts, (before, gains), refs = refs[:8], refs[8:10], refs[10:]
    outs, others, buffer, sems, upstreams, more = refs[11:]
    downs = fetch(1, refs[:11], buffer, sems)
    ups = fetch(0, refs[:11], buffer, sems)
    for copy in downs.values():
        copy.start()
    rows, hidden = before.shape
    width = buffer.shape[1]
    loads = []
    for at in range(8):
        row = at // 4 * 4 + (ids[2] ^ FLIPS[at % 4])
        loads.append(pltpu.make_async_copy(parts[at], upstreams.at[:, row], more.at[at]))
        loads[-1].start()
    for copy in loads:
        copy.wait()
    total = jnp.zeros((rows, hidden), F32)
    for at in range(8):
        downs[at].wait()
        ups[at].start()
        block = ids[0] ^ at
        upstream = upstreams[block].reshape(rows, width)
        total = total + dot(upstream, buffer[8 + at], 1, 0)
    value = before[...]
    square = value * value
    bend = jnp.tanh(GELU_C * value * (1.0 + GELU_A * square))
    slope = 0.5 * (1.0 + bend) + 0.5 * GELU_C * value * (1.0 - bend * bend) * (
        1.0 + 3.0 * GELU_A * square
    )
    grad16 = (total * slope).astype(BF16)
    grad = grad16.astype(F32)
    first = jnp.sum(grad * gains[...], axis=1, keepdims=True)
    second = jnp.sum(grad * value, axis=1, keepdims=True)
    lane = lax.broadcasted_iota(jnp.int32, (rows, TAIL), 1)
    tail = jnp.where(lane == 0, first, jnp.where(lane == 1, second, 0.0))
    for copy in ups.values():
        copy.wait()
    if not split:
        others[...] = tail
        for at in range(8):
            outs[ids[0] ^ at] = dot(grad16, buffer[at], 1, 1)
        return
    for ref, core in ((others, 1 - ids[1]), (outs, ids[1])):
        for at in range(4):
            block = at // 2 * 4 + core * 2 + at % 2
            value = dot(grad16, buffer[ids[0] ^ block], 1, 1)
            ref[at // 2, at % 2, :, :width] = value.astype(ref.dtype)
            ref[at // 2, at % 2, :, width:] = tail.astype(ref.dtype)


def call(kernel, name, shapes, operands, weights=(), more=(), places=None):
    scratch = []
    if weights:
        scratch.append(pltpu.VMEM((16,) + weights[0].shape[1:], BF16))
        scratch.append(pltpu.SemaphoreType.DMA((16,)))
    scratch.extend(more)
    flops = 2 * 256 * 224 * 960 * 16 if weights else 0
    return pl.pallas_call(
        kernel,
        out_shape=shapes,
        in_specs=[SMEM] + (places or [VMEM] * (len(operands) - 1)) + [ANY] * len(weights),
        out_specs=tuple(VMEM for _ in shapes),
        scratch_shapes=scratch,
        compiler_params=PARAMS,
        cost_estimate=pl.CostEstimate(
            flops=flops, bytes_accessed=MEBIBYTES[name] << 20, transcendentals=0
        ),
        name=name,
    )(*operands, *weights)


def norm_stats(rows, axes):
    mean = jnp.mean(rows, axis=axes, keepdims=True)
    centered = rows - mean
    return mean, lax.rsqrt(jnp.mean(centered * centered, axis=axes, keepdims=True) + EPS)


def packed(data, sums):
    high = lax.reduce_precision(sums, 8, 7)
    tail = jnp.concatenate([high, sums - high], -1).astype(BF16)
    return jnp.concatenate([data.astype(BF16), jnp.broadcast_to(tail, data.shape[:-1] + (4,))], -1)


def unpacked(payload, cols):
    payload = payload.astype(F32)
    sums = payload[0, :, cols : cols + 2] + payload[0, :, cols + 2 : cols + 4]
    return payload[..., :cols], sums


def norm_back(grad, sums, rows, mean, inverse, gain, features):
    normed = (rows - mean) * inverse
    first, second = sums[:, 0:1] / features, sums[:, 1:2] / features
    return inverse * (grad * gain - first - normed * second)


def unit_rows(embed):
    inv = lax.rsqrt(jnp.sum(embed * embed, axis=1, keepdims=True) + EPS)
    return inv, (embed * inv).astype(BF16)


def unit_back(embed, inv, grad):
    along = jnp.sum(embed * grad, axis=1, keepdims=True)
    return inv * (grad - embed * (inv * inv) * along)


def gelu16(before):
    return jax.nn.gelu(before, approximate=True).astype(BF16)


def gelu_back16(before, grad):
    _, back = jax.vjp(lambda value: jax.nn.gelu(value, approximate=True), before)
    return back(grad)[0].astype(BF16)


def shards(
    image_in,
    text_in,
    image_gain,
    text_gain,
    image_up,
    image_down,
    text_up,
    text_down,
    image_head,
    log_scale,
    bias,
):
    img, grp = lax.axis_index("img"), lax.axis_index("grp")
    x, core = grp // 2, grp % 2
    members = lax.axis_size("img")
    top = members // 2
    rows, image_cols = image_in.shape
    quarter = rows // 4
    text_cols = text_in.shape[1]
    image_features, text_features = image_cols * 4, text_cols * 4
    width = image_features // members
    share_count = members // 4
    hidden_half = image_up.shape[1] // 2
    embed_width = image_head.shape[1]
    scale = jnp.exp(log_scale[0])
    shift = bias[0]
    ids = jnp.stack([img // top * 4 + img % 4, core, grp]).astype(jnp.int32)

    gate = lax.optimization_barrier

    with jax.named_scope("first"):
        shard = jnp.stack([image_up, image_down.T])
        low, high = shard[..., :hidden_half], shard[..., hidden_half:]
        both_halves = gate(jnp.stack([low, high]))
        far = widen(exchange(both_halves, img), img)
        near = widen(take(both_halves, img // top), img)
        near_y, near_z = swap(near, "img", 1), swap(near, "img", 2)
        own_in = image_in.reshape(rows, share_count, width).transpose(1, 0, 2)
        far_in = swap(own_in, "img", top)
        text_x = swap(text_in, "grp", 2)
        text_parts = [text_in, text_x, swap(text_in, "grp", 1), swap(text_x, "grp", 1)]
        text_parts = place(text_parts, grp, FLIPS)
        text_whole = text_parts.transpose(1, 0, 2).reshape(rows, text_features).astype(F32)
        text_mean, text_inverse = norm_stats(text_whole, 1)
        text_normed = (text_whole - text_mean) * text_inverse
        text_before = dot((text_normed * text_gain).astype(BF16), text_up, 1, 0)
        text_branch = dot(gelu16(text_before), text_down, 1, 0)
        text_branch = text_branch.reshape(2, 2, quarter, text_features)
        send = take(text_branch, 1 - core, 1).astype(BF16)
        total = take(text_branch, core, 1) + swap(send, "grp", 1).astype(F32)
        send = take(total, 1 - x).astype(BF16)
        total = take(total, x) + swap(send, "grp", 2).astype(F32)
        head_x = swap(image_head, "grp", 2)
        near_last = swap(near_z, "img", 1)
        gain = image_gain.reshape(members, 1, width)
        text_gains = jnp.sum(text_up.astype(F32) * text_gain[:, None], axis=0)
        own_gain = lax.dynamic_slice_in_dim(text_gain, grp * text_cols, text_cols, 0)
        ready = (ids, gain, text_gains, own_gain, scale, shift)
        far, near_y, near_z, near_last, total, far_in, head_x, ready = gate(
            (far, near_y, near_z, near_last, total, far_in, head_x, ready)
        )
        ids, gain, text_gains, own_gain, scale, shift = ready

    with jax.named_scope("second"):
        far_parts, total = gate(([far[0], far[1]], total))
        far_y = [swap(part, "img", 1) for part in far_parts]
        far_z = [swap(part, "img", 2) for part in far_parts]
        both = jnp.concatenate([own_in, far_in], 1)
        both_x = swap(both, "grp", 2)
        total = tie(total, both_x)
        far_y, far_z, both, both_x = gate((far_y, far_z, both, both_x))
        parts = [both, both_x, swap(both, "grp", 1), swap(both_x, "grp", 1)]
        scaled, own_rows, mean, inverse = call(
            norm_kernel,
            "norm",
            (
                jax.ShapeDtypeStruct((members, 2 * rows + 16, width), BF16),
                jax.ShapeDtypeStruct((members, quarter, width), BF16),
                jax.ShapeDtypeStruct((2 * rows, 1), F32),
                jax.ShapeDtypeStruct((2 * rows, 1), F32),
            ),
            (ids, *parts, gain),
        )
        scaled = blocked(scaled)

    with jax.named_scope("third"):
        far_last = [swap(far_z[0], "img", 1), swap(far_y[1], "img", 2)]
        weights = [near, near_y, near_z, far, near_last]
        for at in (0, 1):
            weights += [far_y[at], far_z[at], far_last[at]]
        text_embed = lax.dynamic_slice_in_dim(text_whole, grp * quarter, quarter, 0) + total
        text_inv, text_unit = unit_rows(text_embed)
        copies = jnp.broadcast_to(text_unit, (top,) + text_unit.shape)
        lines = [list(range(first, members, 2)) for first in (0, 1)]
        line = lax.all_to_all(
            copies, "img", split_axis=0, concat_axis=0, tiled=True, axis_index_groups=lines
        )
        other = swap(line, "img", 1)
        odd = img % 2 == 1
        share = jnp.stack([jnp.where(odd, other, line), jnp.where(odd, line, other)], 1)
        share = share.reshape(members * quarter, embed_width)
        at = jnp.arange(members * quarter, dtype=jnp.int32)
        share_ids = at // quarter * rows + at % quarter
        text_ids = jnp.concatenate([share_ids + (grp ^ flip) * quarter for flip in FLIPS])

    with jax.named_scope("norm"):
        share_x = swap(share, "grp", 2)
        every = [share, share_x, swap(share, "grp", 1), swap(share_x, "grp", 1)]
        every_text = jnp.concatenate(every)

    with jax.named_scope("image_forward"):
        shape = (8, 4, quarter, image_features // 8)
        (partial,) = call(
            up_kernel,
            "up",
            (jax.ShapeDtypeStruct((2 * rows + 16, hidden_half), F32),),
            (ids, scaled),
            weights[:7] + [weights[6]] * 4,
        )
        head_x = tie(head_x, partial)
        heads = [image_head, head_x, swap(image_head, "grp", 1), swap(head_x, "grp", 1)]
        head = place(heads, grp, FLIPS).reshape(members, width, embed_width)
        before, gains, keep, send = call(
            forward_kernel,
            "forward",
            (
                jax.ShapeDtypeStruct((2 * rows, hidden_half), F32),
                jax.ShapeDtypeStruct((1, hidden_half), F32),
                jax.ShapeDtypeStruct(shape, F32),
                jax.ShapeDtypeStruct(shape, BF16),
            ),
            (ids, scaled, tie(partial, share)),
            weights,
        )
        total = (keep + swap(send, "grp", 1).astype(F32)).reshape(8, 2, 2, quarter, -1)
        send = tie(take(total, 1 - x, 2).astype(BF16), share_x)
        got = swap(send, "grp", 2)
        total = take(total, x, 2) + got.astype(F32)
        branch = total[:, 0] + swap(total[:, 1].astype(BF16), "img", top).astype(F32)
        image_mid16 = (own_rows.astype(F32) + in_order(branch, members)).astype(BF16)
        image_mid16 = image_mid16.transpose(1, 0, 2).reshape(quarter, image_features)
        image_embed = dot(image_mid16, head.reshape(image_features, embed_width), 1, 0)
        image_inv, image_unit = unit_rows(image_embed)

    with jax.named_scope("image_loss"):
        image_ids = img * rows + grp * quarter + jnp.arange(quarter, dtype=jnp.int32)
        logits = scale * dot(image_unit, every_text, 1, 1) + shift
        same = (image_ids[:, None] == text_ids[None, :]).astype(F32)
        pull = (jax.nn.sigmoid(logits) - same).astype(BF16)
        grad_image_unit = scale * dot(pull, every_text, 1, 0)
        grad_embed16 = unit_back(image_embed, image_inv, grad_image_unit).astype(BF16)
        grad_mid16 = dot(grad_embed16, head.reshape(image_features, embed_width), 1, 1)
        grad_mid16 = grad_mid16.astype(BF16).reshape(quarter, members, width)
        grad_mid16 = blocked(grad_mid16.transpose(1, 0, 2))

    with jax.named_scope("text_loss"):
        unit_x = tie(swap(image_unit, "grp", 2), grad_embed16)
        pair = jnp.stack([image_unit, unit_x])
        image_units = jnp.concatenate([pair, swap(pair, "grp", 1)]).reshape(rows, embed_width)
        image_units = tie(image_units, grad_mid16)
        logits = scale * dot(image_units, share, 1, 1) + shift
        at = jnp.arange(quarter, dtype=jnp.int32)
        group_ids = jnp.concatenate([img * rows + (grp ^ flip) * quarter + at for flip in FLIPS])
        same = (group_ids[:, None] == (share_ids + grp * quarter)[None, :]).astype(F32)
        pull = (jax.nn.sigmoid(logits) - same).astype(BF16)
        text_partial = (scale * dot(pull, image_units, 0, 0)).astype(BF16)
        text_partial = text_partial.reshape(members, quarter, embed_width)
        text_parts = lax.all_to_all(
            text_partial, "img", split_axis=0, concat_axis=0, tiled=True
        )

    with jax.named_scope("image_backward"):
        far_grad = tie(swap(grad_mid16, "img", top), text_partial)
        sides = []
        for part in (grad_mid16, far_grad):
            part_x = swap(part, "grp", 2)
            sides += [part, part_x, swap(part, "grp", 1), swap(part_x, "grp", 1)]
        split = members == 8
        if split:
            shape = (2, share_count, 2 * rows, width + TAIL)
            shapes = (jax.ShapeDtypeStruct(shape, F32), jax.ShapeDtypeStruct(shape, BF16))
        else:
            shapes = (
                jax.ShapeDtypeStruct((8, 2 * rows, image_features // 8), F32),
                jax.ShapeDtypeStruct((2 * rows, TAIL), F32),
            )
        keep, send = call(
            functools.partial(back_kernel, split),
            "back",
            shapes,
            (ids, *sides, before, gains),
            weights,
            [
                pltpu.VMEM((8, 8, quarter, image_features // 8), BF16),
                pltpu.SemaphoreType.DMA((8,)),
            ],
            [ANY] * 8 + [VMEM, VMEM],
        )
        if not split:
            tail = jnp.broadcast_to(send, (members,) + send.shape)
            total = jnp.concatenate([in_order(keep, members), tail], -1)
            total = total.reshape(2, 2, share_count, 2 * rows, width + TAIL)
            keep, send = take(total, core, 1), take(total, 1 - core, 1).astype(BF16)
        total = keep + tie(swap(send, "grp", 1), text_parts).astype(F32)
        send = take(total, 1 - x).astype(BF16)
        text_parts, send, own_parts = gate((text_parts, send, sides[:4]))
        total = take(total, x) + swap(send, "grp", 2).astype(F32)
        got = swap(total[:, rows:].astype(BF16), "img", top).astype(F32)
        total = total[:, :rows] + got
        total, sums = total[..., :width], total[0, :, width : width + 2]
        back = norm_back(
            total,
            sums,
            own_in.astype(F32),
            mean[:rows],
            inverse[:rows],
            take(gain.reshape(4, share_count, 1, width), grp),
            image_features,
        )
        own_grad = [
            take(in_order(part, members).reshape(4, share_count, quarter, width), grp)
            for part in own_parts
        ]
        own_grad = place(own_grad, grp, FLIPS).transpose(1, 0, 2, 3)
        own_grad = own_grad.reshape(share_count, rows, width)
        image_grad = (own_grad.astype(F32) + back).astype(BF16)
        image_grad = jnp.concatenate([image_grad[at] for at in range(share_count)], 1)

    with jax.named_scope("text_sum"):
        grad_text_unit = jnp.sum(text_parts.astype(F32), axis=0)
        grad_text16 = unit_back(text_embed, text_inv, grad_text_unit).astype(BF16)

    with jax.named_scope("text_backward"):
        pair = jnp.stack([grad_text16, swap(grad_text16, "grp", 2)])
        parts = jnp.concatenate([pair, swap(pair, "grp", 1)])
        upstream = place([parts[at] for at in range(4)], grp, FLIPS).reshape(rows, text_features)
        grad_before = gelu_back16(text_before, dot(upstream, text_down, 1, 1))
        grad32 = grad_before.astype(F32)
        sums = jnp.stack([jnp.sum(grad32 * text_gains, 1), jnp.sum(grad32 * text_before, 1)], 1)
        blocks = text_up.reshape(4, text_cols, -1)
        partial = {flip: dot(grad_before, take(blocks, grp ^ flip), 1, 1) for flip in FLIPS}
        send = jnp.stack([packed(partial[flip], sums) for flip in (1, 3)])
        data, more = unpacked(swap(send, "grp", 1), text_cols)
        sums = sums + more
        send = packed(partial[2] + data[1], sums)[None]
        more_data, more = unpacked(swap(send, "grp", 2), text_cols)
        total, sums = partial[0] + data[0] + more_data[0], sums + more
        back = norm_back(
            total, sums, text_in.astype(F32), text_mean, text_inverse, own_gain, text_features
        )
        own_grad = lax.dynamic_slice_in_dim(upstream, grp * text_cols, text_cols, 1)
        text_grad = (own_grad.astype(F32) + back).astype(BF16)
    return (image_grad, text_grad)


def solution(mesh):
    in_specs = (
        P("img", "grp"),
        P("img", "grp"),
        P(),
        P(),
        P("img", "grp"),
        P("grp", "img"),
        P(None, "grp"),
        P("grp", None),
        P("grp", None),
        P(),
        P(),
    )
    out_specs = (P("img", "grp"), P("img", "grp"))
    return jax.shard_map(shards, mesh=mesh, in_specs=in_specs, out_specs=out_specs, check_vma=False)
```
